512 devices in a mesh: ctx: 128 (over x, z, core), head: 4 (over y).
Axes of the slice: x: 4, y: 4, z: 16, core: 2. Of those that a mesh axis runs over, the one named last changes fastest.
Arguments:
- queries: bfloat16 [16, 32768, 128], P('head', 'ctx'), may hold values from -6 to 6
- key_vectors: bfloat16 [16, 32768, 128], P('head', 'ctx'), may hold values from -6 to 6
- value_vectors: bfloat16 [16, 32768, 128], P('head', 'ctx'), may hold values from -12 to 12
- norm_gain: float32 [16, 128], P('head'), may hold values from 0.5 to 1.5
- upstream: bfloat16 [16, 32768, 128], P('head', 'ctx'), may hold values from -6 to 6
- cluster_ids: int32 [16, 32768, 1], P('head', 'ctx'), may hold values from 0 to 255; in each aligned block of 256 rows (0 to 255, 256 to 511, ..., all dimensions but the last counted through in order) at most 2 rows name the same one
- positions: int32 [32768], P('ctx'), may hold values from 0 to 32767, each once
Outputs:
- normed_out: bfloat16 [16, 32768, 128], P('head', 'ctx')
- grad_queries: bfloat16 [16, 32768, 128], P('head', 'ctx')
- grad_keys: bfloat16 [16, 32768, 128], P('head', 'ctx')
- grad_values: bfloat16 [16, 32768, 128], P('head', 'ctx')
- centroids: float32 [256, 16, 128], P('ctx', 'head')
The draws below stay inside these ranges and needn't reach their ends.
Inputs may be any that keep to these rules, and one draw needn't show every extreme that they name: `cluster_ids`: within one head, the 256 tokens of one index of ctx name one cluster at most 2 times. `positions`: every position appears once.
All inputs are finite; a program needn't handle non-finite values.
Results may differ from the reference program's by a relative error of at most 0.02.
Values may be sent and summed in bfloat16 or wider, within the bound.
No kernel may reach another device: no remote copies, remote signals or barrier semaphores. Data moves between devices by JAX's collectives and lax.ppermute only.
A program may use at most 64 MiB of HBM per device.

```python
import math
import jax
import jax.numpy as jnp
import numpy as np
from jax import lax

HEADS = 16
DH = 128
CLUSTERS = 256
TOK_DEV = 256
SEND_CAP = 2
TOKENS = 32768
ROWS = 256
N_CTX = 128


def draw_queries(key, part):
    key = jax.random.fold_in(key, 1)
    shape_full = (HEADS, TOKENS, DH)
    return jnp.clip(jax.random.normal(key, shape_full), -4.0, 4.0).astype(jnp.bfloat16)


def draw_key_vectors(key, part):
    key = jax.random.fold_in(key, 2)
    shape_full = (HEADS, TOKENS, DH)
    return jnp.clip(jax.random.normal(key, shape_full), -4.0, 4.0).astype(jnp.bfloat16)


def draw_value_vectors(key, part):
    key = jax.random.fold_in(key, 3)
    shape_full = (HEADS, TOKENS, DH)
    head_scale = (0.3 * 10.0 ** (jnp.arange(HEADS, dtype=jnp.float32) / max(HEADS - 1, 1))).reshape(HEADS, 1, 1)
    return (jnp.clip(jax.random.normal(key, shape_full), -4.0, 4.0) * head_scale).astype(jnp.bfloat16)


def block_levels(stream_key, extent, shards, low, high):
    loudness = 1.0
    for dim, blocks in shards:
        draws = jax.random.uniform(jax.random.fold_in(jax.random.fold_in(stream_key, 6), dim), (blocks,), jnp.float32, low / len(shards), high / len(shards))
        loudness = loudness * jnp.repeat(jnp.exp(draws), extent[dim] // blocks).reshape((-1,) + (1,) * (len(extent) - 1 - dim))
    return loudness


def deal_out(stream_key, own, number, rows, number_of, top, reach, skew):
    ranking = jax.random.permutation(stream_key, number_of)
    crowded, ordinary = shares(number_of, rows * top, reach, skew, True), shares(number_of, rows * top, reach, skew, False)
    places = jnp.arange(number_of)

    def named(lengths, rotation):
        used = int((lengths > 0).sum())
        fixed = max(1, used // 4)
        shifted = fixed + (places - fixed + rotation * (used - fixed)) % max(1, number_of - fixed)
        return jnp.zeros((number_of,), jnp.int32).at[ranking[jnp.where(places < fixed, places, shifted)]].set(jnp.asarray(lengths, jnp.int32))

    lengths = jnp.where(number % 4 == 0, named(crowded, number // 4), named(ordinary, number - number // 4 - 1))
    mixed = jax.random.permutation(jax.random.fold_in(own, 3), number_of)
    donor, taker = mixed[0:number_of // 2 * 2:2], mixed[1:number_of // 2 * 2:2]
    margin = jnp.minimum(lengths[donor] - 1, reach - lengths[taker]) // 2
    margin = jnp.where((donor == ranking[0]) | (taker == ranking[0]) | (lengths[taker] == 0), 0, jnp.maximum(margin, 0))
    shifted = jax.random.randint(jax.random.fold_in(own, 4), (number_of // 2,), 0, 1 << 20) % (margin + 1)
    lengths = lengths.at[donor].add(-shifted).at[taker].add(shifted)
    labels = jnp.searchsorted(jnp.cumsum(lengths), jnp.arange(rows * top), side="right").astype(jnp.int32)
    grid = labels.reshape(top, rows).T
    grid = grid[jax.random.permutation(jax.random.fold_in(own, 1), rows)]
    rotation = jax.random.randint(jax.random.fold_in(own, 2), (rows, 1), 0, top)
    return jnp.take_along_axis(grid, (jnp.arange(top)[None, :] + rotation) % top, axis=1)


def shares(amount, total, bound, slope, full):
    portions = [(1 << 20) // math.isqrt(rank ** slope) + 1 for rank in range(1, amount + 1)]
    largest = bound if full else min(bound, max(-(-total // amount), total * portions[0] // sum(portions)))
    least = 1 if total - largest >= amount - 1 else 0
    counts, spare = [largest] + [least] * (amount - 1), total - largest - least * (amount - 1)
    while spare > 0:
        candidates = [i for i in range(1, amount) if counts[i] < largest] or [i for i in range(1, amount) if counts[i] < bound]
        pool, remaining = sum([portions[i] for i in candidates]), spare
        for i in candidates:
            extra = min(bound - counts[i], max(1, remaining * portions[i] // pool), spare)
            counts[i] = counts[i] + extra
            spare = spare - extra
    return np.array(counts)


def centred(key, dims, deviation, most, split=(), kind=jnp.bfloat16):
    entries = deviation * jax.random.normal(key, dims, jnp.float32)
    if split:
        entries = entries * block_levels(key, dims, split, -0.22, 0.18)
    return jnp.clip(entries, -most, most).astype(kind)


def setup_inputs(seed: int = 0) -> dict:
    keys = jax.random.split(jax.random.key(seed), 8)
    queries = draw_queries(jax.random.fold_in(keys[7], 71), 0)
    key_vectors = draw_key_vectors(jax.random.fold_in(keys[7], 71), 0)
    value_vectors = draw_value_vectors(jax.random.fold_in(keys[7], 71), 0)
    norm_gain = jnp.clip(1.0 + 0.1 * jax.random.normal(keys[3], (HEADS, DH), jnp.float32), 0.5, 1.5)
    upstream = centred(keys[4], (HEADS, TOKENS, DH), 1.0, 6.0, ((0, 4), (1, 128)))
    cluster_ids_keys = jax.random.split(jax.random.fold_in(keys[5], 1), HEADS * TOKENS // TOK_DEV)
    cluster_ids_turns = jax.random.permutation(jax.random.fold_in(keys[5], 3), HEADS * TOKENS // TOK_DEV)
    cluster_ids = jax.vmap(lambda own, number: deal_out(jax.random.fold_in(keys[5], 2), own, number, TOK_DEV, CLUSTERS, 1, SEND_CAP, 2))(cluster_ids_keys, cluster_ids_turns).reshape((HEADS, TOKENS, 1))
    positions = jax.random.permutation(keys[6], TOKENS).astype(jnp.int32)
    return {"queries": queries, "key_vectors": key_vectors, "value_vectors": value_vectors, "norm_gain": norm_gain, "upstream": upstream, "cluster_ids": cluster_ids, "positions": positions}


def slot_of(member):
    blocked = member.reshape(N_CTX, TOK_DEV)
    matches = blocked[:, :, None] == blocked[:, None, :]
    earlier = lax.broadcasted_iota(jnp.int32, (TOK_DEV, TOK_DEV), 0) > lax.broadcasted_iota(jnp.int32, (TOK_DEV, TOK_DEV), 1)
    rank_rows = lax.optimization_barrier(jnp.sum(jnp.logical_and(matches, earlier[None]), axis=2, dtype=jnp.int32)).reshape(TOKENS)
    device_of = jnp.arange(TOKENS, dtype=jnp.int32) // TOK_DEV
    return (device_of * SEND_CAP + rank_rows).astype(jnp.int32)

def place(source, member, slot_row, filler):
    shape_full = (CLUSTERS, ROWS) + source.shape[1:]
    return jnp.full(shape_full, filler, source.dtype).at[member, slot_row].set(source)

def softmax_weights(query_block, key_block, slot_pos, factor):
    scores = jnp.einsum('crd,cjd->crj', query_block.astype(jnp.float32), key_block.astype(jnp.float32)) * factor
    allowed = jnp.logical_and(slot_pos[:, None, :] >= 0, slot_pos[:, None, :] <= slot_pos[:, :, None])
    scores = jnp.where(allowed, scores, -1e+30)
    highest = lax.optimization_barrier(jnp.max(scores, axis=2, keepdims=True))
    exponent = jnp.exp(scores - highest)
    return exponent / lax.optimization_barrier(jnp.sum(exponent, axis=2, keepdims=True))

def attend(query_block, key_block, value_block, slot_pos, factor):
    weights = softmax_weights(query_block, key_block, slot_pos, factor)
    rounded = weights.astype(jnp.bfloat16)
    return jnp.einsum('crj,cjd->crd', rounded.astype(jnp.float32), value_block.astype(jnp.float32)).astype(jnp.bfloat16)

def attend_back(query_block, key_block, value_block, slot_pos, grad_block, out_block, factor):
    weights = softmax_weights(query_block, key_block, slot_pos, factor)
    rounded = weights.astype(jnp.bfloat16).astype(jnp.float32)
    grad_wide = grad_block.astype(jnp.float32)
    delta_row = lax.optimization_barrier(jnp.sum(grad_wide * out_block.astype(jnp.float32), axis=2))
    grad_value = jnp.einsum('crj,crd->cjd', rounded, grad_wide).astype(jnp.bfloat16)
    grad_prob = jnp.einsum('crd,cjd->crj', grad_wide, value_block.astype(jnp.float32))
    grad_score = (factor * weights * (grad_prob - delta_row[:, :, None])).astype(jnp.bfloat16).astype(jnp.float32)
    grad_query = jnp.einsum('crj,cjd->crd', grad_score, key_block.astype(jnp.float32)).astype(jnp.bfloat16)
    grad_key = jnp.einsum('crj,crd->cjd', grad_score, query_block.astype(jnp.float32)).astype(jnp.bfloat16)
    return (grad_query, grad_key, grad_value)

def reference(queries, key_vectors, value_vectors, norm_gain, upstream, cluster_ids, positions):
    factor = DH ** (-0.5)
    member_all = cluster_ids[:, :, 0]

    def forward_head(packed):
        query_head, key_head, value_head, member = packed
        slot_row = slot_of(member)
        pos_block = place(positions, member, slot_row, -1)
        out_block = attend(place(query_head, member, slot_row, 0), place(key_head, member, slot_row, 0), place(value_head, member, slot_row, 0), pos_block, factor)
        return out_block[member, slot_row]
    attention = lax.map(forward_head, (queries, key_vectors, value_vectors, member_all)).astype(jnp.float32)
    width_all = HEADS * DH
    squares = lax.optimization_barrier(jnp.sum(attention * attention, axis=(0, 2)))
    inverse = lax.rsqrt(squares / width_all + 1e-06)[None, :, None]
    gain_full = norm_gain[:, None, :]
    normed_out = (attention * inverse * gain_full).astype(jnp.bfloat16)
    scaled_grad = gain_full * upstream.astype(jnp.float32)
    dot_total = lax.optimization_barrier(jnp.sum(scaled_grad * attention, axis=(0, 2)))
    grad_attention = (inverse * scaled_grad - attention * inverse * inverse * inverse * dot_total[None, :, None] / width_all).astype(jnp.bfloat16)

    def backward_head(packed):
        query_head, key_head, value_head, member, grad_head = packed
        slot_row = slot_of(member)
        pos_block = place(positions, member, slot_row, -1)
        query_block = place(query_head, member, slot_row, 0)
        key_block = place(key_head, member, slot_row, 0)
        value_block = place(value_head, member, slot_row, 0)
        out_block = attend(query_block, key_block, value_block, pos_block, factor)
        grad_block = place(grad_head, member, slot_row, 0)
        grad_query, grad_key, grad_value = attend_back(query_block, key_block, value_block, pos_block, grad_block, out_block, factor)
        return (grad_query[member, slot_row], grad_key[member, slot_row], grad_value[member, slot_row])
    grad_queries, grad_keys, grad_values = lax.map(backward_head, (queries, key_vectors, value_vectors, member_all, grad_attention))

    def sum_head(key_head, member):
        return jax.ops.segment_sum(key_head.astype(jnp.float32), member, num_segments=CLUSTERS)
    cluster_sums = jnp.transpose(jax.vmap(sum_head)(key_vectors, member_all), (1, 0, 2))
    centroids = cluster_sums * lax.rsqrt(lax.optimization_barrier(jnp.mean(cluster_sums * cluster_sums, axis=2, keepdims=True)) + 1e-06)
    return (normed_out, grad_queries, grad_keys, grad_values, centroids)
```

```python
import jax
import jax.numpy as jnp
from jax import lax
from jax.sharding import PartitionSpec as P

CLUSTERS = 256
SEND_CAP = 2


def rank_within(member):
    tok_count = member.shape[1]
    matches = member[:, :, None] == member[:, None, :]
    earlier = lax.broadcasted_iota(jnp.int32, (tok_count, tok_count), 0) > lax.broadcasted_iota(
        jnp.int32, (tok_count, tok_count), 1
    )
    return jnp.sum(jnp.logical_and(matches, earlier[None]), axis=2, dtype=jnp.int32)


def weights_of(query_block, key_block, slot_pos, factor):
    scores = (
        jnp.einsum("urd,ujd->urj", query_block, key_block, preferred_element_type=jnp.float32)
        * factor
    )
    allowed = jnp.logical_and(
        slot_pos[:, None, :] >= 0, slot_pos[:, None, :] <= slot_pos[:, :, None]
    )
    scores = jnp.where(allowed, scores, -1e30)
    highest = jnp.max(scores, axis=2, keepdims=True)
    exponent = jnp.exp(scores - highest)
    return exponent / jnp.sum(exponent, axis=2, keepdims=True)


def local(queries, key_vectors, value_vectors, norm_gain, upstream, cluster_ids, positions):
    heads, tokens, feature = queries.shape
    n_ctx = lax.axis_size("ctx")
    per_dev = CLUSTERS // n_ctx
    factor = feature ** (-0.5)
    member = cluster_ids[:, :, 0]
    target = member * SEND_CAP + rank_within(member)
    slots = CLUSTERS * SEND_CAP
    mine = slots // n_ctx
    onehot = (
        target[:, None, :] == lax.broadcasted_iota(jnp.int32, (1, slots, 1), 1)
    )
    place = onehot.astype(jnp.bfloat16)

    def to_owner(source):
        placed = jnp.einsum(
            "hst,htd->hsd", place, source, preferred_element_type=jnp.float32
        ).astype(jnp.bfloat16)
        placed = placed.reshape(heads, n_ctx, mine, source.shape[2])
        placed = placed.transpose(1, 0, 2, 3).reshape(n_ctx, heads * mine, source.shape[2])
        return lax.all_to_all(placed, "ctx", 0, 0, tiled=True)

    def from_owner(block):
        back = lax.all_to_all(block, "ctx", 0, 0, tiled=True)
        back = back.reshape(n_ctx, heads, mine, block.shape[2])
        back = back.transpose(1, 0, 2, 3).reshape(heads, slots, block.shape[2])
        return jnp.einsum(
            "hst,hsd->htd", place, back, preferred_element_type=jnp.float32
        ).astype(jnp.bfloat16)

    def units(recv):
        width = recv.shape[2]
        block = recv.reshape(n_ctx, heads * per_dev, SEND_CAP, width).transpose(1, 0, 2, 3)
        return block.reshape(heads * per_dev, n_ctx * SEND_CAP, width)

    def ununits(block):
        width = block.shape[2]
        recv = block.reshape(heads * per_dev, n_ctx, SEND_CAP, width).transpose(1, 0, 2, 3)
        return recv.reshape(n_ctx, heads * mine, width)

    pos_slots = jnp.sum(
        jnp.where(onehot, positions[None, None, :] + 1, 0), axis=2, dtype=jnp.int32
    ) - 1
    pos_slots = pos_slots.reshape(heads, n_ctx, mine).transpose(1, 0, 2).reshape(n_ctx, heads * mine)
    pos_recv = lax.all_to_all(pos_slots, "ctx", 0, 0, tiled=True)
    slot_pos = units(pos_recv[:, :, None])[:, :, 0]
    recv = to_owner(jnp.concatenate([queries, key_vectors, value_vectors], axis=2))
    block = units(recv)
    query_own, key_own, value_own = (
        block[:, :, :feature], block[:, :, feature : 2 * feature], block[:, :, 2 * feature :]
    )
    weights = weights_of(query_own, key_own, slot_pos, factor)
    rounded = weights.astype(jnp.bfloat16)
    out_own = jnp.einsum(
        "urj,ujd->urd", rounded, value_own, preferred_element_type=jnp.float32
    ).astype(jnp.bfloat16)
    attention = from_owner(ununits(out_own)).astype(jnp.float32)
    width_all = heads * feature * lax.axis_size("head")
    gain_full = norm_gain[:, None, :]
    scaled_grad = gain_full * upstream.astype(jnp.float32)
    sums = lax.psum(
        jnp.stack(
            [
                jnp.sum(attention * attention, axis=(0, 2)),
                jnp.sum(scaled_grad * attention, axis=(0, 2)),
            ]
        ),
        "head",
    )
    inverse = lax.rsqrt(sums[0] / width_all + 1e-06)[None, :, None]
    dot_total = sums[1][None, :, None]
    normed_out = (attention * inverse * gain_full).astype(jnp.bfloat16)
    grad_attention = (
        inverse * scaled_grad
        - attention * inverse * inverse * inverse * dot_total / width_all
    ).astype(jnp.bfloat16)
    grad_block = units(to_owner(grad_attention))
    delta_row = jnp.sum(grad_block.astype(jnp.float32) * out_own.astype(jnp.float32), axis=2)
    grad_value = jnp.einsum(
        "urj,urd->ujd", rounded, grad_block, preferred_element_type=jnp.float32
    ).astype(jnp.bfloat16)
    grad_prob = jnp.einsum(
        "urd,ujd->urj", grad_block, value_own, preferred_element_type=jnp.float32
    )
    grad_score = (factor * weights * (grad_prob - delta_row[:, :, None])).astype(jnp.bfloat16)
    grad_query = jnp.einsum(
        "urj,ujd->urd", grad_score, key_own, preferred_element_type=jnp.float32
    ).astype(jnp.bfloat16)
    grad_key = jnp.einsum(
        "urj,urd->ujd", grad_score, query_own, preferred_element_type=jnp.float32
    ).astype(jnp.bfloat16)
    grads = from_owner(ununits(jnp.concatenate([grad_query, grad_key, grad_value], axis=2)))
    cluster_sums = jnp.sum(key_own.astype(jnp.float32), axis=1)
    cluster_sums = cluster_sums.reshape(heads, per_dev, feature).transpose(1, 0, 2)
    centroids = cluster_sums * lax.rsqrt(
        jnp.mean(cluster_sums * cluster_sums, axis=2, keepdims=True) + 1e-06
    )
    return (
        normed_out,
        grads[:, :, :feature],
        grads[:, :, feature : 2 * feature],
        grads[:, :, 2 * feature :],
        centroids,
    )


def solution(mesh):
    tok = P("head", "ctx", None)
    in_specs = (tok, tok, tok, P("head", None), tok, tok, P("ctx"))
    out_specs = (tok, tok, tok, tok, P("ctx", "head", None))
    return jax.shard_map(local, mesh=mesh, in_specs=in_specs, out_specs=out_specs, check_vma=False)
```

```python
import jax
import jax.numpy as jnp
from jax import lax
from jax.sharding import PartitionSpec as P

CLUSTERS = 256
SEND_CAP = 2
PACKED = 13
GROUP = 16


def rank_within(member):
    tok_count = member.shape[1]
    matches = member[:, :, None] == member[:, None, :]
    earlier = lax.broadcasted_iota(jnp.int32, (tok_count, tok_count), 0) > lax.broadcasted_iota(
        jnp.int32, (tok_count, tok_count), 1
    )
    return jnp.sum(jnp.logical_and(matches, earlier[None]), axis=2, dtype=jnp.int32)


def weights_of(query_block, key_block, slot_pos, factor):
    scores = (
        jnp.einsum("urd,ujd->urj", query_block, key_block, preferred_element_type=jnp.float32)
        * factor
    )
    allowed = jnp.logical_and(
        slot_pos[:, None, :] >= 0, slot_pos[:, None, :] <= slot_pos[:, :, None]
    )
    scores = jnp.where(allowed, scores, -1e30)
    highest = jnp.max(scores, axis=2, keepdims=True)
    exponent = jnp.exp(scores - highest)
    return exponent / jnp.sum(exponent, axis=2, keepdims=True)


def dense(queries, key_vectors, value_vectors, norm_gain, upstream, cluster_ids, positions):
    heads, tokens, feature = queries.shape
    n_ctx = lax.axis_size("ctx")
    per_dev = CLUSTERS // n_ctx
    factor = feature ** (-0.5)
    member = cluster_ids[:, :, 0]
    target = member * SEND_CAP + rank_within(member)
    slots = CLUSTERS * SEND_CAP
    mine = slots // n_ctx
    onehot = (
        target[:, None, :] == lax.broadcasted_iota(jnp.int32, (1, slots, 1), 1)
    )
    place = onehot.astype(jnp.bfloat16)

    def to_owner(source):
        placed = jnp.einsum(
            "hst,htd->hsd", place, source, preferred_element_type=jnp.float32
        ).astype(jnp.bfloat16)
        placed = placed.reshape(heads, n_ctx, mine, source.shape[2])
        placed = placed.transpose(1, 0, 2, 3).reshape(n_ctx, heads * mine, source.shape[2])
        return lax.all_to_all(placed, "ctx", 0, 0, tiled=True)

    def from_owner(block):
        back = lax.all_to_all(block, "ctx", 0, 0, tiled=True)
        back = back.reshape(n_ctx, heads, mine, block.shape[2])
        back = back.transpose(1, 0, 2, 3).reshape(heads, slots, block.shape[2])
        return jnp.einsum(
            "hst,hsd->htd", place, back, preferred_element_type=jnp.float32
        ).astype(jnp.bfloat16)

    def units(recv):
        width = recv.shape[2]
        block = recv.reshape(n_ctx, heads * per_dev, SEND_CAP, width).transpose(1, 0, 2, 3)
        return block.reshape(heads * per_dev, n_ctx * SEND_CAP, width)

    def ununits(block):
        width = block.shape[2]
        recv = block.reshape(heads * per_dev, n_ctx, SEND_CAP, width).transpose(1, 0, 2, 3)
        return recv.reshape(n_ctx, heads * mine, width)

    pos_slots = jnp.sum(
        jnp.where(onehot, positions[None, None, :] + 1, 0), axis=2, dtype=jnp.int32
    ) - 1
    pos_slots = pos_slots.reshape(heads, n_ctx, mine).transpose(1, 0, 2).reshape(n_ctx, heads * mine)
    pos_recv = lax.all_to_all(pos_slots, "ctx", 0, 0, tiled=True)
    slot_pos = units(pos_recv[:, :, None])[:, :, 0]
    recv = to_owner(jnp.concatenate([queries, key_vectors, value_vectors], axis=2))
    block = units(recv)
    query_own, key_own, value_own = (
        block[:, :, :feature], block[:, :, feature : 2 * feature], block[:, :, 2 * feature :]
    )
    weights = weights_of(query_own, key_own, slot_pos, factor)
    rounded = weights.astype(jnp.bfloat16)
    out_own = jnp.einsum(
        "urj,ujd->urd", rounded, value_own, preferred_element_type=jnp.float32
    ).astype(jnp.bfloat16)
    attention = from_owner(ununits(out_own)).astype(jnp.float32)
    width_all = heads * feature * lax.axis_size("head")
    gain_full = norm_gain[:, None, :]
    scaled_grad = gain_full * upstream.astype(jnp.float32)
    sums = lax.psum(
        jnp.stack(
            [
                jnp.sum(attention * attention, axis=(0, 2)),
                jnp.sum(scaled_grad * attention, axis=(0, 2)),
            ]
        ),
        "head",
    )
    inverse = lax.rsqrt(sums[0] / width_all + 1e-06)[None, :, None]
    dot_total = sums[1][None, :, None]
    normed_out = (attention * inverse * gain_full).astype(jnp.bfloat16)
    grad_attention = (
        inverse * scaled_grad
        - attention * inverse * inverse * inverse * dot_total / width_all
    ).astype(jnp.bfloat16)
    grad_block = units(to_owner(grad_attention))
    delta_row = jnp.sum(grad_block.astype(jnp.float32) * out_own.astype(jnp.float32), axis=2)
    grad_value = jnp.einsum(
        "urj,urd->ujd", rounded, grad_block, preferred_element_type=jnp.float32
    ).astype(jnp.bfloat16)
    grad_prob = jnp.einsum(
        "urd,ujd->urj", grad_block, value_own, preferred_element_type=jnp.float32
    )
    grad_score = (factor * weights * (grad_prob - delta_row[:, :, None])).astype(jnp.bfloat16)
    grad_query = jnp.einsum(
        "urj,ujd->urd", grad_score, key_own, preferred_element_type=jnp.float32
    ).astype(jnp.bfloat16)
    grad_key = jnp.einsum(
        "urj,urd->ujd", grad_score, query_own, preferred_element_type=jnp.float32
    ).astype(jnp.bfloat16)
    grads = from_owner(ununits(jnp.concatenate([grad_query, grad_key, grad_value], axis=2)))
    cluster_sums = jnp.sum(key_own.astype(jnp.float32), axis=1)
    cluster_sums = cluster_sums.reshape(heads, per_dev, feature).transpose(1, 0, 2)
    centroids = cluster_sums * lax.rsqrt(
        jnp.mean(cluster_sums * cluster_sums, axis=2, keepdims=True) + 1e-06
    )
    return (
        normed_out,
        grads[:, :, :feature],
        grads[:, :, feature : 2 * feature],
        grads[:, :, 2 * feature :],
        centroids,
    )


def packed(queries, key_vectors, value_vectors, norm_gain, upstream, cluster_ids, positions):
    heads, tokens, feature = queries.shape
    n_ctx = lax.axis_size("ctx")
    per_dev = CLUSTERS // n_ctx
    units = heads * per_dev
    slots = units * SEND_CAP
    groups = n_ctx // GROUP
    shift = n_ctx // heads
    factor = feature ** (-0.5)
    all_tok = heads * tokens
    member = cluster_ids[:, :, 0]
    head_of = lax.broadcasted_iota(jnp.int32, member.shape, 0)
    owner = (member // per_dev + shift * head_of) % n_ctx
    unit = head_of * per_dev + member % per_dev
    order = (owner * units + unit) * tokens + lax.broadcasted_iota(jnp.int32, member.shape, 1)
    order = order.reshape(all_tok)
    owner = owner.reshape(all_tok)
    below = order[None, :] < order[:, None]
    place = jnp.sum(
        jnp.logical_and(below, order[None, :] >= owner[:, None] * (units * tokens)),
        axis=1,
        dtype=jnp.int32,
    )
    rank = jnp.sum(
        jnp.logical_and(below, order[None, :] >= order[:, None] // tokens * tokens),
        axis=1,
        dtype=jnp.int32,
    )
    slot = unit.reshape(all_tok) * SEND_CAP + rank
    crowded = jnp.any(place >= PACKED)
    row = jnp.where(place < PACKED, owner * PACKED + place, -1)
    scatter = (
        row[None, :] == lax.broadcasted_iota(jnp.int32, (n_ctx * PACKED, 1), 0)
    ).astype(jnp.bfloat16)
    pos_all = jnp.broadcast_to(positions[None, :], member.shape).reshape(all_tok)
    notes = jnp.stack([slot + 1, pos_all // 256, pos_all % 256], axis=1).astype(jnp.bfloat16)
    source = jnp.concatenate([queries, key_vectors, value_vectors], axis=2)
    source = jnp.concatenate([source.reshape(all_tok, 3 * feature), notes], axis=1)
    sent = jnp.einsum("rt,td->rd", scatter, source, preferred_element_type=jnp.float32)
    sent = sent.astype(jnp.bfloat16)
    notes_row = sent[:, 3 * feature :].reshape(n_ctx, 1, 3 * PACKED)
    flag = jnp.broadcast_to(crowded, (n_ctx, 1, 1)).astype(jnp.bfloat16)
    notes_row = jnp.concatenate([notes_row, flag], axis=2)
    notes_row = jnp.pad(notes_row, ((0, 0), (0, 0), (0, feature - 3 * PACKED - 1)))
    message = sent[:, : 3 * feature].reshape(n_ctx, 3 * PACKED, feature)
    recv = lax.all_to_all(
        jnp.concatenate([message, notes_row], axis=1), "ctx", 0, 0, tiled=True
    )
    notes_recv = recv[:, 3 * PACKED, :]
    any_crowded = jnp.max(notes_recv[:, 3 * PACKED].astype(jnp.float32))
    notes_recv = notes_recv[:, : 3 * PACKED].reshape(n_ctx, PACKED, 3)
    slot_recv = notes_recv[:, :, 0].reshape(groups, 1, GROUP * PACKED).astype(jnp.int32) - 1
    rows_shape = (1, slots * GROUP, 1)
    cols_shape = (1, 1, GROUP * PACKED)
    row_id = lax.broadcasted_iota(jnp.int32, rows_shape, 1)
    col_src = lax.broadcasted_iota(jnp.int32, cols_shape, 2) // PACKED
    spread = jnp.logical_and(
        slot_recv == row_id // GROUP, col_src == row_id % GROUP
    ).astype(jnp.bfloat16)
    valid = (notes_recv[:, :, :1] > 0).astype(jnp.bfloat16)
    packed_rows = jnp.concatenate(
        [recv[:, : 3 * PACKED].reshape(n_ctx, PACKED, 3 * feature), notes_recv[:, :, 1:], valid],
        axis=2,
    ).reshape(groups, GROUP * PACKED, 3 * feature + 3)
    block = jnp.einsum("grk,gkd->grd", spread, packed_rows, preferred_element_type=jnp.float32)

    def by_unit(rows):
        rows = rows.reshape(groups, units, SEND_CAP, GROUP, rows.shape[2])
        return rows.transpose(1, 2, 0, 3, 4).reshape(units, SEND_CAP * n_ctx, rows.shape[4])

    def from_units(block):
        width = block.shape[2]
        rows = block.reshape(units, SEND_CAP, groups, GROUP, width).transpose(2, 0, 1, 3, 4)
        rows = rows.reshape(groups, slots * GROUP, width)
        rows = jnp.einsum("grk,grd->gkd", spread, rows, preferred_element_type=jnp.float32)
        return rows.astype(jnp.bfloat16)

    def home(rows, count):
        back = lax.all_to_all(rows, "ctx", 0, 0, tiled=True)
        back = back.reshape(n_ctx * PACKED, count * feature)
        return jnp.einsum(
            "rt,rd->td", scatter, back, preferred_element_type=jnp.float32
        ).reshape(heads, tokens, count * feature)

    pos_rows = by_unit(block[:, :, 3 * feature :])
    slot_pos = (
        pos_rows[:, :, 0] * 256.0 + pos_rows[:, :, 1] + pos_rows[:, :, 2] - 1.0
    ).astype(jnp.int32)
    block = by_unit(block[:, :, : 3 * feature].astype(jnp.bfloat16))
    query_own, key_own, value_own = (
        block[:, :, :feature], block[:, :, feature : 2 * feature], block[:, :, 2 * feature :]
    )
    weights = weights_of(query_own, key_own, slot_pos, factor)
    rounded = weights.astype(jnp.bfloat16)
    out_own = jnp.einsum(
        "urj,ujd->urd", rounded, value_own, preferred_element_type=jnp.float32
    ).astype(jnp.bfloat16)
    attention = home(from_units(out_own).reshape(n_ctx, PACKED, feature), 1)
    width_all = heads * feature * lax.axis_size("head")
    gain_full = norm_gain[:, None, :]
    scaled_grad = gain_full * upstream.astype(jnp.float32)
    sums = lax.psum(
        jnp.stack(
            [
                jnp.sum(attention * attention, axis=(0, 2)),
                jnp.sum(scaled_grad * attention, axis=(0, 2)),
                jnp.broadcast_to(any_crowded, (tokens,)),
            ]
        ),
        "head",
    )
    inverse = lax.rsqrt(sums[0] / width_all + 1e-06)[None, :, None]
    dot_total = sums[1][None, :, None]
    normed_out = (attention * inverse * gain_full).astype(jnp.bfloat16)
    grad_attention = (
        inverse * scaled_grad
        - attention * inverse * inverse * inverse * dot_total / width_all
    ).astype(jnp.bfloat16)
    grad_rows = jnp.einsum(
        "rt,td->rd", scatter, grad_attention.reshape(all_tok, feature),
        preferred_element_type=jnp.float32,
    ).astype(jnp.bfloat16)
    grad_recv = lax.all_to_all(
        grad_rows.reshape(n_ctx, PACKED, feature), "ctx", 0, 0, tiled=True
    ).reshape(groups, GROUP * PACKED, feature)
    grad_block = by_unit(
        jnp.einsum("grk,gkd->grd", spread, grad_recv, preferred_element_type=jnp.float32)
        .astype(jnp.bfloat16)
    )
    delta_row = jnp.sum(grad_block.astype(jnp.float32) * out_own.astype(jnp.float32), axis=2)
    grad_value = jnp.einsum(
        "urj,urd->ujd", rounded, grad_block, preferred_element_type=jnp.float32
    ).astype(jnp.bfloat16)
    grad_prob = jnp.einsum(
        "urd,ujd->urj", grad_block, value_own, preferred_element_type=jnp.float32
    )
    grad_score = (factor * weights * (grad_prob - delta_row[:, :, None])).astype(jnp.bfloat16)
    grad_query = jnp.einsum(
        "urj,ujd->urd", grad_score, key_own, preferred_element_type=jnp.float32
    ).astype(jnp.bfloat16)
    grad_key = jnp.einsum(
        "urj,urd->ujd", grad_score, query_own, preferred_element_type=jnp.float32
    ).astype(jnp.bfloat16)
    back = from_units(jnp.concatenate([grad_query, grad_key, grad_value], axis=2))
    grads = home(back.reshape(n_ctx, 3 * PACKED, feature), 3).astype(jnp.bfloat16)
    own_sums = jnp.sum(key_own.astype(jnp.float32), axis=1).reshape(heads, per_dev, feature)
    moved = [
        lax.ppermute(
            own_sums[i], "ctx", [(d, (d - shift * i) % n_ctx) for d in range(n_ctx)]
        )
        for i in range(1, heads)
    ]
    cluster_sums = jnp.stack([own_sums[0]] + moved, axis=1)
    centroids = cluster_sums * lax.rsqrt(
        jnp.mean(cluster_sums * cluster_sums, axis=2, keepdims=True) + 1e-06
    )
    outs = (
        normed_out,
        grads[:, :, :feature],
        grads[:, :, feature : 2 * feature],
        grads[:, :, 2 * feature :],
        centroids,
    )
    return outs, sums[2, 0] > 0


def local(*args):
    outs, crowded = packed(*args)
    return lax.cond(crowded, lambda given, made: dense(*given), lambda given, made: made, args, outs)


def solution(mesh):
    tok = P("head", "ctx", None)
    in_specs = (tok, tok, tok, P("head", None), tok, tok, P("ctx"))
    out_specs = (tok, tok, tok, tok, P("ctx", "head", None))
    return jax.shard_map(local, mesh=mesh, in_specs=in_specs, out_specs=out_specs, check_vma=False)
```

```python
import functools

import jax
import jax.numpy as jnp
from jax import lax
from jax.experimental import pallas as pl
from jax.experimental.pallas import tpu as pltpu
from jax.sharding import PartitionSpec as P

CLUSTERS = 256
SEND_CAP = 2
PACKED = 13
GROUP = 16
HEAD_SHIFT = 32
FLAG_LANE = 48


def rank_within(member):
    tok_count = member.shape[1]
    matches = member[:, :, None] == member[:, None, :]
    earlier = lax.broadcasted_iota(jnp.int32, (tok_count, tok_count), 0) > lax.broadcasted_iota(
        jnp.int32, (tok_count, tok_count), 1
    )
    return jnp.sum(jnp.logical_and(matches, earlier[None]), axis=2, dtype=jnp.int32)


def weights_of(query_block, key_block, slot_pos, factor):
    scores = (
        jnp.einsum("urd,ujd->urj", query_block, key_block, preferred_element_type=jnp.float32)
        * factor
    )
    allowed = jnp.logical_and(
        slot_pos[:, None, :] >= 0, slot_pos[:, None, :] <= slot_pos[:, :, None]
    )
    scores = jnp.where(allowed, scores, -1e30)
    highest = jnp.max(scores, axis=2, keepdims=True)
    exponent = jnp.exp(scores - highest)
    return exponent / jnp.sum(exponent, axis=2, keepdims=True)


def dense(queries, key_vectors, value_vectors, norm_gain, upstream, cluster_ids, positions):
    heads, tokens, feature = queries.shape
    n_ctx = lax.axis_size("ctx")
    per_dev = CLUSTERS // n_ctx
    factor = feature ** (-0.5)
    member = cluster_ids[:, :, 0]
    target = member * SEND_CAP + rank_within(member)
    slots = CLUSTERS * SEND_CAP
    mine = slots // n_ctx
    onehot = (
        target[:, None, :] == lax.broadcasted_iota(jnp.int32, (1, slots, 1), 1)
    )
    place = onehot.astype(jnp.bfloat16)

    def to_owner(source):
        placed = jnp.einsum(
            "hst,htd->hsd", place, source, preferred_element_type=jnp.float32
        ).astype(jnp.bfloat16)
        placed = placed.reshape(heads, n_ctx, mine, source.shape[2])
        placed = placed.transpose(1, 0, 2, 3).reshape(n_ctx, heads * mine, source.shape[2])
        return lax.all_to_all(placed, "ctx", 0, 0, tiled=True)

    def from_owner(block):
        back = lax.all_to_all(block, "ctx", 0, 0, tiled=True)
        back = back.reshape(n_ctx, heads, mine, block.shape[2])
        back = back.transpose(1, 0, 2, 3).reshape(heads, slots, block.shape[2])
        return jnp.einsum(
            "hst,hsd->htd", place, back, preferred_element_type=jnp.float32
        ).astype(jnp.bfloat16)

    def units(recv):
        width = recv.shape[2]
        block = recv.reshape(n_ctx, heads * per_dev, SEND_CAP, width).transpose(1, 0, 2, 3)
        return block.reshape(heads * per_dev, n_ctx * SEND_CAP, width)

    def ununits(block):
        width = block.shape[2]
        recv = block.reshape(heads * per_dev, n_ctx, SEND_CAP, width).transpose(1, 0, 2, 3)
        return recv.reshape(n_ctx, heads * mine, width)

    pos_slots = jnp.sum(
        jnp.where(onehot, positions[None, None, :] + 1, 0), axis=2, dtype=jnp.int32
    ) - 1
    pos_slots = pos_slots.reshape(heads, n_ctx, mine).transpose(1, 0, 2).reshape(n_ctx, heads * mine)
    pos_recv = lax.all_to_all(pos_slots, "ctx", 0, 0, tiled=True)
    slot_pos = units(pos_recv[:, :, None])[:, :, 0]
    recv = to_owner(jnp.concatenate([queries, key_vectors, value_vectors], axis=2))
    block = units(recv)
    query_own, key_own, value_own = (
        block[:, :, :feature], block[:, :, feature : 2 * feature], block[:, :, 2 * feature :]
    )
    weights = weights_of(query_own, key_own, slot_pos, factor)
    rounded = weights.astype(jnp.bfloat16)
    out_own = jnp.einsum(
        "urj,ujd->urd", rounded, value_own, preferred_element_type=jnp.float32
    ).astype(jnp.bfloat16)
    attention = from_owner(ununits(out_own)).astype(jnp.float32)
    width_all = heads * feature * lax.axis_size("head")
    gain_full = norm_gain[:, None, :]
    scaled_grad = gain_full * upstream.astype(jnp.float32)
    sums = lax.psum(
        jnp.stack(
            [
                jnp.sum(attention * attention, axis=(0, 2)),
                jnp.sum(scaled_grad * attention, axis=(0, 2)),
            ]
        ),
        "head",
    )
    inverse = lax.rsqrt(sums[0] / width_all + 1e-06)[None, :, None]
    dot_total = sums[1][None, :, None]
    normed_out = (attention * inverse * gain_full).astype(jnp.bfloat16)
    grad_attention = (
        inverse * scaled_grad
        - attention * inverse * inverse * inverse * dot_total / width_all
    ).astype(jnp.bfloat16)
    grad_block = units(to_owner(grad_attention))
    delta_row = jnp.sum(grad_block.astype(jnp.float32) * out_own.astype(jnp.float32), axis=2)
    grad_value = jnp.einsum(
        "urj,urd->ujd", rounded, grad_block, preferred_element_type=jnp.float32
    ).astype(jnp.bfloat16)
    grad_prob = jnp.einsum(
        "urd,ujd->urj", grad_block, value_own, preferred_element_type=jnp.float32
    )
    grad_score = (factor * weights * (grad_prob - delta_row[:, :, None])).astype(jnp.bfloat16)
    grad_query = jnp.einsum(
        "urj,ujd->urd", grad_score, key_own, preferred_element_type=jnp.float32
    ).astype(jnp.bfloat16)
    grad_key = jnp.einsum(
        "urj,urd->ujd", grad_score, query_own, preferred_element_type=jnp.float32
    ).astype(jnp.bfloat16)
    grads = from_owner(ununits(jnp.concatenate([grad_query, grad_key, grad_value], axis=2)))
    cluster_sums = jnp.sum(key_own.astype(jnp.float32), axis=1)
    cluster_sums = cluster_sums.reshape(heads, per_dev, feature).transpose(1, 0, 2)
    centroids = cluster_sums * lax.rsqrt(
        jnp.mean(cluster_sums * cluster_sums, axis=2, keepdims=True) + 1e-06
    )
    return (
        normed_out,
        grads[:, :, :feature],
        grads[:, :, feature : 2 * feature],
        grads[:, :, 2 * feature :],
        centroids,
    )


def iota(shape, dim):
    return lax.broadcasted_iota(jnp.int32, shape, dim)


def dot(a, b, contract=((1,), (0,))):
    return lax.dot_general(a, b, (contract, ((), ())), preferred_element_type=jnp.float32)


def to_columns(rows):
    width = rows[0].shape[1]
    stacked = jnp.concatenate([r.astype(jnp.float32) for r in rows], axis=0)
    filler = jnp.zeros((128 - len(rows), width), jnp.float32)
    return jnp.transpose(jnp.concatenate([stacked, filler], axis=0))


def to_tiles(rows, note):
    sub = iota((GROUP, 8, 128), 1)
    first, second, third = (r[:, 8:, :] for r in rows)
    third = jnp.where(sub == 5, note, third)
    tile_a = jnp.where(sub < 5, first, pltpu.roll(third, 5, 1))
    tile_b = jnp.where(sub < 5, second, pltpu.roll(third, 2, 1))
    return jnp.concatenate([r[:, :8, :] for r in rows] + [tile_a, tile_b], axis=1)


def from_tiles(message):
    tiles = [message[:, 8 * i : 8 * i + 8, :] for i in range(5)]
    sub = iota((GROUP, 8, 128), 1)
    third = jnp.where(sub < 3, pltpu.roll(tiles[3], 3, 1), pltpu.roll(tiles[4], 6, 1))
    parts = [(tiles[0], tiles[3]), (tiles[1], tiles[4]), (tiles[2], third)]
    rows = [jnp.concatenate(p, axis=1).reshape(GROUP * 16, 128) for p in parts]
    return jnp.concatenate(rows, axis=1).astype(jnp.bfloat16), tiles[4]


def send_kernel(ids_ref, pos_ref, q_ref, k_ref, v_ref, msg_ref, row_ref, col_ref, src_ref):
    heads, tokens = ids_ref.shape
    all_tok = heads * tokens
    lane = iota((1, tokens), 1)
    owners, units, orders = [], [], []
    for h in range(heads):
        ids = ids_ref[h : h + 1, :]
        owner = ((ids >> 1) + HEAD_SHIFT * h) & 127
        unit = 2 * h + (ids & 1)
        owners.append(owner)
        units.append(unit)
        orders.append((owner * 8 + unit) * tokens + lane)
    order = jnp.concatenate(orders, axis=1)
    owner = jnp.concatenate(owners, axis=1)
    unit = jnp.concatenate(units, axis=1)
    order_col = to_columns([order])[:, 0:1].astype(jnp.int32)
    base = owner * (8 * tokens)
    place = jnp.zeros((1, all_tok), jnp.int32)
    for c in range(all_tok // 128):
        other = order_col[c * 128 : (c + 1) * 128, :]
        hit = jnp.logical_and(other < order, other >= base)
        place = place + jnp.sum(jnp.where(hit, 1, 0), axis=0, keepdims=True)
    ranks = []
    for h in range(heads):
        other = order_col[h * tokens : (h + 1) * tokens, :]
        hit = jnp.logical_and(other < orders[h], other >= orders[h] - lane)
        ranks.append(jnp.sum(jnp.where(hit, 1, 0), axis=0, keepdims=True))
    slot = unit * 2 + jnp.concatenate(ranks, axis=1)
    row = jnp.where(place < PACKED, owner * 16 + place, -1)
    row_ref[...] = row
    crowded = jnp.where(jnp.max(place) >= PACKED, 1.0, 0.0)
    pos = jnp.concatenate([pos_ref[...]] * heads, axis=1)
    cols = to_columns([place, slot + 16, (pos >> 8) + 1, pos & 255, row])
    col_ref[...] = cols[:, 4:5].astype(jnp.int32)
    lanes = iota((all_tok, 128), 1).astype(jnp.float32)
    slot_col = cols[:, 1:2]
    notes = jnp.where(lanes == cols[:, 0:1], slot_col - 15.0, 0.0)
    notes = notes + jnp.where(lanes == slot_col, cols[:, 2:3], 0.0)
    notes = notes + jnp.where(lanes == slot_col + 16.0, cols[:, 3:4], 0.0)
    for i, ref in enumerate((q_ref, k_ref, v_ref)):
        src_ref[:, i * 128 : (i + 1) * 128] = ref[...].reshape(all_tok, 128)
    src_ref[:, 384:512] = notes.astype(jnp.bfloat16)
    flag = jnp.where(iota((1, 1, 128), 2) == FLAG_LANE, crowded, 0.0)

    def step(c):
        at = c * GROUP
        pick = jnp.where(iota((256, all_tok), 0) + at * 16 == row, 1.0, 0.0).astype(jnp.bfloat16)
        got = dot(pick, src_ref[...]).reshape(GROUP, 16, 512)
        rows = [got[:, :, i * 128 : (i + 1) * 128] for i in range(3)]
        note = jnp.sum(got[:, :, 384:512], axis=1, keepdims=True) + flag
        msg_ref[pl.ds(at, GROUP)] = to_tiles(rows, note).astype(jnp.bfloat16)

    for c in range(128 // GROUP):
        step(c)


def put_units(ref, which, at, rows):
    for s in range(16):
        piece = rows[s * GROUP : (s + 1) * GROUP, :]
        ref[which, s // 2, pl.ds((s % 2) * 128 + at, GROUP), :] = piece


def take_units(ref, which, at):
    return jnp.concatenate(
        [ref[which, s // 2, pl.ds((s % 2) * 128 + at, GROUP), :] for s in range(16)], axis=0
    )


def forward_kernel(
    factor, msg_ref, out_msg_ref, qkv_ref, own_ref, prob_ref, spread_ref, sums_ref, flag_ref, note_ref
):
    repeat = (iota((128, 256), 0) == iota((128, 256), 1) % 16).astype(jnp.float32)
    repeat = repeat.astype(jnp.bfloat16)
    r0, r1 = iota((256, 256), 0), iota((256, 256), 1)
    want = (r0 // GROUP + 1).astype(jnp.float32)
    same = r1 // 16 == r0 % GROUP
    sub = iota((GROUP, 8, 128), 1)

    def unpack(g):
        at = g * GROUP
        rows, last = from_tiles(msg_ref[pl.ds(at, GROUP)].astype(jnp.float32))
        note = jnp.sum(jnp.where(sub == 7, last, 0.0), axis=1)
        note_ref[pl.ds(at, GROUP), :] = note
        slot = dot(note.astype(jnp.bfloat16), repeat)
        slot = jnp.concatenate([slot] * 16, axis=0)
        spread = jnp.where(jnp.logical_and(slot == want, same), 1.0, 0.0).astype(jnp.bfloat16)
        spread_ref[g] = spread
        block = dot(spread, rows).astype(jnp.bfloat16)
        for i in range(3):
            put_units(qkv_ref, i, at, block[:, i * 128 : (i + 1) * 128])

    for g in range(128 // GROUP):
        unpack(g)
    note = note_ref[...]
    flag_ref[...] = jnp.max(note, axis=0, keepdims=True)
    pos = jnp.where(note > 0.5, (note - 1.0) * 256.0 + pltpu.roll(note, 112, 1), -1.0)
    pos_t = jnp.transpose(pos)
    for u in range(8):
        a, b = 16 + 2 * u, 17 + 2 * u
        pos_col = jnp.concatenate([pos[:, a : a + 1], pos[:, b : b + 1]], axis=0)
        pos_row = jnp.concatenate([pos_t[a : a + 1, :], pos_t[b : b + 1, :]], axis=1)
        key = qkv_ref[1, u]
        scores = dot(qkv_ref[0, u], key, ((1,), (1,))) * factor
        allowed = jnp.logical_and(pos_row >= 0.0, pos_row <= pos_col)
        scores = jnp.where(allowed, scores, -1e30)
        expo = jnp.exp(scores - jnp.max(scores, axis=1, keepdims=True))
        prob = (expo * (1.0 / jnp.sum(expo, axis=1, keepdims=True))).astype(jnp.bfloat16)
        prob_ref[u] = prob
        own_ref[0, u] = dot(prob, qkv_ref[2, u]).astype(jnp.bfloat16)
        sums_ref[u : u + 1, :] = jnp.sum(key.astype(jnp.float32), axis=0, keepdims=True)

    def pack(g):
        at = g * GROUP
        rows = dot(spread_ref[g], take_units(own_ref, 0, at), ((0,), (0,)))
        out_msg_ref[pl.ds(at, GROUP)] = rows.reshape(GROUP, 16, 128).astype(jnp.bfloat16)

    for g in range(128 // GROUP):
        pack(g)


def backward_kernel(factor, msg_ref, qkv_ref, own_ref, prob_ref, spread_ref, out_msg_ref, grad_ref):
    def unpack(g):
        at = g * GROUP
        rows = msg_ref[pl.ds(at, GROUP)].reshape(GROUP * 16, 128)
        put_units(grad_ref, 0, at, dot(spread_ref[g], rows).astype(jnp.bfloat16))

    for g in range(128 // GROUP):
        unpack(g)
    for u in range(8):
        grad, prob = grad_ref[0, u], prob_ref[u]
        delta = jnp.sum(
            grad.astype(jnp.float32) * own_ref[0, u].astype(jnp.float32), axis=1, keepdims=True
        )
        grad_prob = dot(grad, qkv_ref[2, u], ((1,), (1,)))
        grad_score = (factor * prob.astype(jnp.float32) * (grad_prob - delta)).astype(jnp.bfloat16)
        grad_ref[1, u] = dot(grad_score, qkv_ref[1, u]).astype(jnp.bfloat16)
        grad_ref[2, u] = dot(grad_score, qkv_ref[0, u], ((0,), (0,))).astype(jnp.bfloat16)
        grad_ref[3, u] = dot(prob, grad, ((0,), (0,))).astype(jnp.bfloat16)

    def pack(g):
        at = g * GROUP
        rows = jnp.concatenate([take_units(grad_ref, i, at) for i in (1, 2, 3)], axis=1)
        rows = dot(spread_ref[g], rows, ((0,), (0,))).reshape(GROUP, 16, 384)
        rows = [rows[:, :, i * 128 : (i + 1) * 128] for i in range(3)]
        none = jnp.zeros((GROUP, 1, 128), jnp.float32)
        out_msg_ref[pl.ds(at, GROUP)] = to_tiles(rows, none).astype(jnp.bfloat16)

    for g in range(128 // GROUP):
        pack(g)


def home_kernel(msg_ref, col_ref, q_ref, k_ref, v_ref, rows_ref):
    for g in range(128 // GROUP):
        rows, _ = from_tiles(msg_ref[pl.ds(g * GROUP, GROUP)].astype(jnp.float32))
        rows_ref[g * 256 : (g + 1) * 256, :] = rows
    heads, tokens, _ = q_ref.shape
    for h in range(heads):
        col = col_ref[h * tokens : (h + 1) * tokens, :]
        pick = jnp.where(iota((tokens, 2048), 1) == col, 1.0, 0.0).astype(jnp.bfloat16)
        got = dot(pick, rows_ref[...]).astype(jnp.bfloat16)
        for i, ref in enumerate((q_ref, k_ref, v_ref)):
            ref[h] = got[:, i * 128 : (i + 1) * 128]


def call(kernel, outs, scratch, *args):
    return pl.pallas_call(
        kernel,
        out_shape=[jax.ShapeDtypeStruct(s, t) for s, t in outs],
        scratch_shapes=[pltpu.VMEM(s, t) for s, t in scratch],
        compiler_params=pltpu.CompilerParams(vmem_limit_bytes=28 * 1024 * 1024),
    )(*args)


def packed(queries, key_vectors, value_vectors, norm_gain, upstream, cluster_ids, positions):
    heads, tokens, feature = queries.shape
    n_ctx = lax.axis_size("ctx")
    per_dev = CLUSTERS // n_ctx
    units = heads * per_dev
    groups = n_ctx // GROUP
    factor = feature ** (-0.5)
    all_tok = heads * tokens
    half, full = jnp.bfloat16, jnp.float32
    message, row, col = call(
        send_kernel,
        [
            ((n_ctx, 40, feature), half),
            ((1, all_tok), jnp.int32),
            ((all_tok, 1), jnp.int32),
        ],
        [((all_tok, 4 * feature), half)],
        cluster_ids.reshape(heads, tokens), positions.reshape(1, tokens),
        queries, key_vectors, value_vectors,
    )
    recv = lax.all_to_all(message, "ctx", 0, 0, tiled=True)
    out_msg, qkv_own, out_own, prob, spread, own_sums, notes = call(
        functools.partial(forward_kernel, factor),
        [
            ((n_ctx, 16, feature), half),
            ((3, units, 256, feature), half),
            ((1, units, 256, feature), half),
            ((units, 256, 256), half),
            ((groups, 256, 256), half),
            ((units, feature), full),
            ((1, feature), full),
        ],
        [((n_ctx, feature), full)],
        recv,
    )
    any_crowded = notes[0, FLAG_LANE]
    back = lax.all_to_all(out_msg, "ctx", 0, 0, tiled=True).reshape(n_ctx * 16, feature)
    scatter = (row == iota((n_ctx * 16, 1), 0)).astype(half)
    attention = jnp.einsum(
        "rt,rd->td", scatter, back, preferred_element_type=full
    ).reshape(heads, tokens, feature).astype(half).astype(full)
    width_all = heads * feature * lax.axis_size("head")
    gain_full = norm_gain[:, None, :]
    scaled_grad = gain_full * upstream.astype(full)
    sums = lax.psum(
        jnp.stack(
            [
                jnp.sum(attention * attention, axis=(0, 2)),
                jnp.sum(scaled_grad * attention, axis=(0, 2)),
                jnp.broadcast_to(any_crowded, (tokens,)),
            ]
        ),
        "head",
    )
    inverse = lax.rsqrt(sums[0] / width_all + 1e-06)[None, :, None]
    dot_total = sums[1][None, :, None]
    normed_out = (attention * inverse * gain_full).astype(half)
    grad_attention = (
        inverse * scaled_grad
        - attention * inverse * inverse * inverse * dot_total / width_all
    ).astype(half)
    grad_rows = jnp.einsum(
        "rt,td->rd", scatter, grad_attention.reshape(all_tok, feature),
        preferred_element_type=full,
    ).astype(half)
    grad_recv = lax.all_to_all(
        grad_rows.reshape(n_ctx, 16, feature), "ctx", 0, 0, tiled=True
    )
    (grad_msg,) = call(
        functools.partial(backward_kernel, factor),
        [((n_ctx, 40, feature), half)],
        [((4, units, 256, feature), half)],
        grad_recv, qkv_own, out_own, prob, spread,
    )
    grads_back = lax.all_to_all(grad_msg, "ctx", 0, 0, tiled=True)
    shape = (heads, tokens, feature)
    grads = call(
        home_kernel, [(shape, half)] * 3, [((n_ctx * 16, 3 * feature), half)], grads_back, col
    )
    own_sums = own_sums.reshape(heads, per_dev, feature)
    moved = [
        lax.ppermute(
            own_sums[i], "ctx", [(d, (d - HEAD_SHIFT * i) % n_ctx) for d in range(n_ctx)]
        )
        for i in range(1, heads)
    ]
    cluster_sums = jnp.stack([own_sums[0]] + moved, axis=1)
    centroids = cluster_sums * lax.rsqrt(
        jnp.mean(cluster_sums * cluster_sums, axis=2, keepdims=True) + 1e-06
    )
    return (normed_out, *grads, centroids), sums[2, 0] > 0


def local(*args):
    outs, crowded = packed(*args)
    return lax.cond(crowded, lambda given, made: dense(*given), lambda given, made: made, args, outs)


def solution(mesh):
    tok = P("head", "ctx", None)
    in_specs = (tok, tok, tok, P("head", None), tok, tok, P("ctx"))
    out_specs = (tok, tok, tok, tok, P("ctx", "head", None))
    return jax.shard_map(local, mesh=mesh, in_specs=in_specs, out_specs=out_specs, check_vma=False)
```

```python
import functools

import jax
import jax.numpy as jnp
from jax import lax
from jax.experimental import pallas as pl
from jax.experimental.pallas import tpu as pltpu
from jax.sharding import PartitionSpec as P

CLUSTERS = 256
SEND_CAP = 2
PACKED = 13
GROUP = 16
HEAD_SHIFT = 32
FLAG_LANE = 48


def rank_within(member):
    tok_count = member.shape[1]
    matches = member[:, :, None] == member[:, None, :]
    earlier = lax.broadcasted_iota(jnp.int32, (tok_count, tok_count), 0) > lax.broadcasted_iota(
        jnp.int32, (tok_count, tok_count), 1
    )
    return jnp.sum(jnp.logical_and(matches, earlier[None]), axis=2, dtype=jnp.int32)


def weights_of(query_block, key_block, slot_pos, factor):
    scores = (
        jnp.einsum("urd,ujd->urj", query_block, key_block, preferred_element_type=jnp.float32)
        * factor
    )
    allowed = jnp.logical_and(
        slot_pos[:, None, :] >= 0, slot_pos[:, None, :] <= slot_pos[:, :, None]
    )
    scores = jnp.where(allowed, scores, -1e30)
    highest = jnp.max(scores, axis=2, keepdims=True)
    exponent = jnp.exp(scores - highest)
    return exponent / jnp.sum(exponent, axis=2, keepdims=True)


def dense(queries, key_vectors, value_vectors, norm_gain, upstream, cluster_ids, positions):
    heads, tokens, feature = queries.shape
    n_ctx = lax.axis_size("ctx")
    per_dev = CLUSTERS // n_ctx
    factor = feature ** (-0.5)
    member = cluster_ids[:, :, 0]
    target = member * SEND_CAP + rank_within(member)
    slots = CLUSTERS * SEND_CAP
    mine = slots // n_ctx
    onehot = (
        target[:, None, :] == lax.broadcasted_iota(jnp.int32, (1, slots, 1), 1)
    )
    place = onehot.astype(jnp.bfloat16)

    def to_owner(source):
        placed = jnp.einsum(
            "hst,htd->hsd", place, source, preferred_element_type=jnp.float32
        ).astype(jnp.bfloat16)
        placed = placed.reshape(heads, n_ctx, mine, source.shape[2])
        placed = placed.transpose(1, 0, 2, 3).reshape(n_ctx, heads * mine, source.shape[2])
        return lax.all_to_all(placed, "ctx", 0, 0, tiled=True)

    def from_owner(block):
        back = lax.all_to_all(block, "ctx", 0, 0, tiled=True)
        back = back.reshape(n_ctx, heads, mine, block.shape[2])
        back = back.transpose(1, 0, 2, 3).reshape(heads, slots, block.shape[2])
        return jnp.einsum(
            "hst,hsd->htd", place, back, preferred_element_type=jnp.float32
        ).astype(jnp.bfloat16)

    def units(recv):
        width = recv.shape[2]
        block = recv.reshape(n_ctx, heads * per_dev, SEND_CAP, width).transpose(1, 0, 2, 3)
        return block.reshape(heads * per_dev, n_ctx * SEND_CAP, width)

    def ununits(block):
        width = block.shape[2]
        recv = block.reshape(heads * per_dev, n_ctx, SEND_CAP, width).transpose(1, 0, 2, 3)
        return recv.reshape(n_ctx, heads * mine, width)

    pos_slots = jnp.sum(
        jnp.where(onehot, positions[None, None, :] + 1, 0), axis=2, dtype=jnp.int32
    ) - 1
    pos_slots = pos_slots.reshape(heads, n_ctx, mine).transpose(1, 0, 2).reshape(n_ctx, heads * mine)
    pos_recv = lax.all_to_all(pos_slots, "ctx", 0, 0, tiled=True)
    slot_pos = units(pos_recv[:, :, None])[:, :, 0]
    recv = to_owner(jnp.concatenate([queries, key_vectors, value_vectors], axis=2))
    block = units(recv)
    query_own, key_own, value_own = (
        block[:, :, :feature], block[:, :, feature : 2 * feature], block[:, :, 2 * feature :]
    )
    weights = weights_of(query_own, key_own, slot_pos, factor)
    rounded = weights.astype(jnp.bfloat16)
    out_own = jnp.einsum(
        "urj,ujd->urd", rounded, value_own, preferred_element_type=jnp.float32
    ).astype(jnp.bfloat16)
    attention = from_owner(ununits(out_own)).astype(jnp.float32)
    width_all = heads * feature * lax.axis_size("head")
    gain_full = norm_gain[:, None, :]
    scaled_grad = gain_full * upstream.astype(jnp.float32)
    sums = lax.psum(
        jnp.stack(
            [
                jnp.sum(attention * attention, axis=(0, 2)),
                jnp.sum(scaled_grad * attention, axis=(0, 2)),
            ]
        ),
        "head",
    )
    inverse = lax.rsqrt(sums[0] / width_all + 1e-06)[None, :, None]
    dot_total = sums[1][None, :, None]
    normed_out = (attention * inverse * gain_full).astype(jnp.bfloat16)
    grad_attention = (
        inverse * scaled_grad
        - attention * inverse * inverse * inverse * dot_total / width_all
    ).astype(jnp.bfloat16)
    grad_block = units(to_owner(grad_attention))
    delta_row = jnp.sum(grad_block.astype(jnp.float32) * out_own.astype(jnp.float32), axis=2)
    grad_value = jnp.einsum(
        "urj,urd->ujd", rounded, grad_block, preferred_element_type=jnp.float32
    ).astype(jnp.bfloat16)
    grad_prob = jnp.einsum(
        "urd,ujd->urj", grad_block, value_own, preferred_element_type=jnp.float32
    )
    grad_score = (factor * weights * (grad_prob - delta_row[:, :, None])).astype(jnp.bfloat16)
    grad_query = jnp.einsum(
        "urj,ujd->urd", grad_score, key_own, preferred_element_type=jnp.float32
    ).astype(jnp.bfloat16)
    grad_key = jnp.einsum(
        "urj,urd->ujd", grad_score, query_own, preferred_element_type=jnp.float32
    ).astype(jnp.bfloat16)
    grads = from_owner(ununits(jnp.concatenate([grad_query, grad_key, grad_value], axis=2)))
    cluster_sums = jnp.sum(key_own.astype(jnp.float32), axis=1)
    cluster_sums = cluster_sums.reshape(heads, per_dev, feature).transpose(1, 0, 2)
    centroids = cluster_sums * lax.rsqrt(
        jnp.mean(cluster_sums * cluster_sums, axis=2, keepdims=True) + 1e-06
    )
    return (
        normed_out,
        grads[:, :, :feature],
        grads[:, :, feature : 2 * feature],
        grads[:, :, 2 * feature :],
        centroids,
    )


def iota(shape, dim):
    return lax.broadcasted_iota(jnp.int32, shape, dim)


def dot(a, b, contract=((1,), (0,))):
    return lax.dot_general(a, b, (contract, ((), ())), preferred_element_type=jnp.float32)


def to_columns(rows):
    width = rows[0].shape[1]
    stacked = jnp.concatenate([r.astype(jnp.float32) for r in rows], axis=0)
    filler = jnp.zeros((128 - len(rows), width), jnp.float32)
    return jnp.transpose(jnp.concatenate([stacked, filler], axis=0))


def to_tiles(rows, note):
    sub = iota((GROUP, 8, 128), 1)
    first, second, third = (r[:, 8:, :] for r in rows)
    third = jnp.where(sub == 5, note, third)
    tile_a = jnp.where(sub < 5, first, pltpu.roll(third, 5, 1))
    tile_b = jnp.where(sub < 5, second, pltpu.roll(third, 2, 1))
    return jnp.concatenate([r[:, :8, :] for r in rows] + [tile_a, tile_b], axis=1)


def from_tiles(message):
    tiles = [message[:, 8 * i : 8 * i + 8, :] for i in range(5)]
    sub = iota((GROUP, 8, 128), 1)
    third = jnp.where(sub < 3, pltpu.roll(tiles[3], 3, 1), pltpu.roll(tiles[4], 6, 1))
    parts = [(tiles[0], tiles[3]), (tiles[1], tiles[4]), (tiles[2], third)]
    rows = [jnp.concatenate(p, axis=1).reshape(GROUP * 16, 128) for p in parts]
    return jnp.concatenate(rows, axis=1).astype(jnp.bfloat16), tiles[4]


def send_kernel(ids_ref, pos_ref, q_ref, k_ref, v_ref, msg_ref, row_ref, col_ref, src_ref):
    heads, tokens = ids_ref.shape
    all_tok = heads * tokens
    lane = iota((1, tokens), 1)
    owners, units, orders = [], [], []
    for h in range(heads):
        ids = ids_ref[h : h + 1, :]
        owner = ((ids >> 1) + HEAD_SHIFT * h) & 127
        unit = 2 * h + (ids & 1)
        owners.append(owner)
        units.append(unit)
        orders.append((owner * 8 + unit) * tokens + lane)
    order = jnp.concatenate(orders, axis=1)
    owner = jnp.concatenate(owners, axis=1)
    unit = jnp.concatenate(units, axis=1)
    order_col = to_columns([order])[:, 0:1].astype(jnp.int32)
    base = owner * (8 * tokens)
    place = jnp.zeros((1, all_tok), jnp.int32)
    for c in range(all_tok // 128):
        other = order_col[c * 128 : (c + 1) * 128, :]
        hit = jnp.logical_and(other < order, other >= base)
        place = place + jnp.sum(jnp.where(hit, 1, 0), axis=0, keepdims=True)
    ranks = []
    for h in range(heads):
        other = order_col[h * tokens : (h + 1) * tokens, :]
        hit = jnp.logical_and(other < orders[h], other >= orders[h] - lane)
        ranks.append(jnp.sum(jnp.where(hit, 1, 0), axis=0, keepdims=True))
    slot = unit * 2 + jnp.concatenate(ranks, axis=1)
    row = jnp.where(place < PACKED, owner * 16 + place, -1)
    row_ref[...] = row
    crowded = jnp.where(jnp.max(place) >= PACKED, 1.0, 0.0)
    pos = jnp.concatenate([pos_ref[...]] * heads, axis=1)
    cols = to_columns([place, slot + 16, (pos >> 8) + 1, pos & 255, row])
    col_ref[...] = cols[:, 4:5].astype(jnp.int32)
    lanes = iota((all_tok, 128), 1).astype(jnp.float32)
    slot_col = cols[:, 1:2]
    notes = jnp.where(lanes == cols[:, 0:1], slot_col - 15.0, 0.0)
    notes = notes + jnp.where(lanes == slot_col, cols[:, 2:3], 0.0)
    notes = notes + jnp.where(lanes == slot_col + 16.0, cols[:, 3:4], 0.0)
    for i, ref in enumerate((q_ref, k_ref, v_ref)):
        src_ref[:, i * 128 : (i + 1) * 128] = ref[...].reshape(all_tok, 128)
    src_ref[:, 384:512] = notes.astype(jnp.bfloat16)
    flag = jnp.where(iota((1, 1, 128), 2) == FLAG_LANE, crowded, 0.0)

    lines = iota((256, all_tok), 0).astype(jnp.float32).astype(jnp.bfloat16)
    one, zero = jnp.ones((), jnp.bfloat16), jnp.zeros((), jnp.bfloat16)

    def step(c):
        at = c * GROUP
        near = row - at * 16
        near = jnp.where(jnp.logical_and(near >= 0, near < 256), near, -1)
        near = near.astype(jnp.float32).astype(jnp.bfloat16)
        pick = jnp.where(lines == near, one, zero)
        got = dot(pick, src_ref[...]).reshape(GROUP, 16, 512)
        rows = [got[:, :, i * 128 : (i + 1) * 128] for i in range(3)]
        note = jnp.sum(got[:, :, 384:512], axis=1, keepdims=True) + flag
        msg_ref[pl.ds(at, GROUP)] = to_tiles(rows, note).astype(jnp.bfloat16)

    for c in range(128 // GROUP):
        step(c)


def put_units(ref, which, at, rows):
    for s in range(16):
        piece = rows[s * GROUP : (s + 1) * GROUP, :]
        ref[which, s // 2, pl.ds((s % 2) * 128 + at, GROUP), :] = piece


def take_units(ref, which, at):
    return jnp.concatenate(
        [ref[which, s // 2, pl.ds((s % 2) * 128 + at, GROUP), :] for s in range(16)], axis=0
    )


def forward_kernel(
    factor, msg_ref, out_msg_hbm, qkv_ref, own_hbm, prob_hbm, spread_ref, sums_ref, flag_ref,
    note_ref, out_msg_ref, own_ref, prob_ref, sems,
):
    repeat = (iota((128, 256), 0) == iota((128, 256), 1) % 16).astype(jnp.float32)
    repeat = repeat.astype(jnp.bfloat16)
    r0, r1 = iota((256, 256), 0), iota((256, 256), 1)
    want = (r0 // GROUP + 1).astype(jnp.float32)
    same = r1 // 16 == r0 % GROUP
    sub = iota((GROUP, 8, 128), 1)

    def unpack(g):
        at = g * GROUP
        rows, last = from_tiles(msg_ref[pl.ds(at, GROUP)].astype(jnp.float32))
        note = jnp.sum(jnp.where(sub == 7, last, 0.0), axis=1)
        note_ref[pl.ds(at, GROUP), :] = note
        slot = dot(note.astype(jnp.bfloat16), repeat)
        slot = jnp.concatenate([slot] * 16, axis=0)
        spread = jnp.where(jnp.logical_and(slot == want, same), 1.0, 0.0).astype(jnp.bfloat16)
        spread_ref[g] = spread
        block = dot(spread, rows).astype(jnp.bfloat16)
        for i in range(3):
            put_units(qkv_ref, i, at, block[:, i * 128 : (i + 1) * 128])

    for g in range(128 // GROUP):
        unpack(g)
    note = note_ref[...]
    flag_ref[...] = jnp.max(note, axis=0, keepdims=True)
    pos = jnp.where(note > 0.5, (note - 1.0) * 256.0 + pltpu.roll(note, 112, 1), -1.0)
    pos_t = jnp.transpose(pos)
    copies = []
    for u in range(8):
        a, b = 16 + 2 * u, 17 + 2 * u
        pos_col = jnp.concatenate([pos[:, a : a + 1], pos[:, b : b + 1]], axis=0)
        pos_row = jnp.concatenate([pos_t[a : a + 1, :], pos_t[b : b + 1, :]], axis=1)
        key = qkv_ref[1, u]
        scores = dot(qkv_ref[0, u], key, ((1,), (1,))) * factor
        allowed = jnp.logical_and(pos_row >= 0.0, pos_row <= pos_col)
        scores = jnp.where(allowed, scores, -1e30)
        expo = jnp.exp(scores - jnp.max(scores, axis=1, keepdims=True))
        prob = (expo * (1.0 / jnp.sum(expo, axis=1, keepdims=True))).astype(jnp.bfloat16)
        prob_ref[u] = prob
        own_ref[0, u] = dot(prob, qkv_ref[2, u]).astype(jnp.bfloat16)
        copies.append(pltpu.make_async_copy(prob_ref.at[u], prob_hbm.at[u], sems.at[0, u]))
        copies[-1].start()
        copies.append(pltpu.make_async_copy(own_ref.at[0, u], own_hbm.at[0, u], sems.at[1, u]))
        copies[-1].start()
        sums_ref[u : u + 1, :] = jnp.sum(key.astype(jnp.float32), axis=0, keepdims=True)

    def pack(g):
        at = g * GROUP
        rows = dot(spread_ref[g], take_units(own_ref, 0, at), ((0,), (0,)))
        out_msg_ref[pl.ds(at, GROUP)] = rows.reshape(GROUP, 16, 128).astype(jnp.bfloat16)
        here = pl.ds(at, GROUP)
        copies.append(
            pltpu.make_async_copy(out_msg_ref.at[here], out_msg_hbm.at[here], sems.at[2, g])
        )
        copies[-1].start()

    for g in range(128 // GROUP):
        pack(g)
    for copy in copies:
        copy.wait()


def backward_kernel(factor, msg_ref, qkv_ref, own_ref, prob_ref, spread_ref, out_msg_ref, grad_ref):
    def unpack(g):
        at = g * GROUP
        rows = msg_ref[pl.ds(at, GROUP)].reshape(GROUP * 16, 128)
        put_units(grad_ref, 0, at, dot(spread_ref[g], rows).astype(jnp.bfloat16))

    for g in range(128 // GROUP):
        unpack(g)
    for u in range(8):
        grad, prob = grad_ref[0, u], prob_ref[u]
        delta = jnp.sum(
            grad.astype(jnp.float32) * own_ref[0, u].astype(jnp.float32), axis=1, keepdims=True
        )
        grad_prob = dot(grad, qkv_ref[2, u], ((1,), (1,)))
        grad_score = (factor * prob.astype(jnp.float32) * (grad_prob - delta)).astype(jnp.bfloat16)
        grad_ref[1, u] = dot(grad_score, qkv_ref[1, u]).astype(jnp.bfloat16)
        grad_ref[2, u] = dot(grad_score, qkv_ref[0, u], ((0,), (0,))).astype(jnp.bfloat16)
        grad_ref[3, u] = dot(prob, grad, ((0,), (0,))).astype(jnp.bfloat16)

    def pack(g):
        at = g * GROUP
        rows = jnp.concatenate([take_units(grad_ref, i, at) for i in (1, 2, 3)], axis=1)
        rows = dot(spread_ref[g], rows, ((0,), (0,))).reshape(GROUP, 16, 384)
        rows = [rows[:, :, i * 128 : (i + 1) * 128] for i in range(3)]
        none = jnp.zeros((GROUP, 1, 128), jnp.float32)
        out_msg_ref[pl.ds(at, GROUP)] = to_tiles(rows, none).astype(jnp.bfloat16)

    for g in range(128 // GROUP):
        pack(g)


def home_kernel(
    msg_ref, col_ref, attn_ref, inv_ref, gain_ref, normed_ref, q_ref, k_ref, v_ref, rows_ref
):
    for g in range(128 // GROUP):
        rows, _ = from_tiles(msg_ref[pl.ds(g * GROUP, GROUP)].astype(jnp.float32))
        rows_ref[g * 256 : (g + 1) * 256, :] = rows
    heads, tokens, _ = q_ref.shape
    for h in range(heads):
        col = col_ref[h * tokens : (h + 1) * tokens, :]
        pick = jnp.where(iota((tokens, 2048), 1) == col, 1.0, 0.0).astype(jnp.bfloat16)
        got = dot(pick, rows_ref[...]).astype(jnp.bfloat16)
        for i, ref in enumerate((q_ref, k_ref, v_ref)):
            ref[h] = got[:, i * 128 : (i + 1) * 128]
        normed = attn_ref[h] * inv_ref[...] * gain_ref[h : h + 1, :]
        normed_ref[h] = normed.astype(jnp.bfloat16)


def call(kernel, outs, scratch, *args, far=(), sems=()):
    spaces = [pltpu.HBM if i in far else pltpu.VMEM for i in range(len(outs))]
    return pl.pallas_call(
        kernel,
        out_shape=[jax.ShapeDtypeStruct(s, t) for s, t in outs],
        out_specs=[pl.BlockSpec(memory_space=space) for space in spaces],
        scratch_shapes=[pltpu.VMEM(s, t) for s, t in scratch]
        + [pltpu.SemaphoreType.DMA(shape) for shape in sems],
        compiler_params=pltpu.CompilerParams(vmem_limit_bytes=28 * 1024 * 1024),
    )(*args)


def packed(queries, key_vectors, value_vectors, norm_gain, upstream, cluster_ids, positions):
    heads, tokens, feature = queries.shape
    n_ctx = lax.axis_size("ctx")
    per_dev = CLUSTERS // n_ctx
    units = heads * per_dev
    groups = n_ctx // GROUP
    factor = feature ** (-0.5)
    all_tok = heads * tokens
    half, full = jnp.bfloat16, jnp.float32
    message, row, col = call(
        send_kernel,
        [
            ((n_ctx, 40, feature), half),
            ((1, all_tok), jnp.int32),
            ((all_tok, 1), jnp.int32),
        ],
        [((all_tok, 4 * feature), half)],
        cluster_ids.reshape(heads, tokens), positions.reshape(1, tokens),
        queries, key_vectors, value_vectors,
    )
    recv = lax.all_to_all(message, "ctx", 0, 0, tiled=True)
    out_msg, qkv_own, out_own, prob, spread, own_sums, notes = call(
        functools.partial(forward_kernel, factor),
        [
            ((n_ctx, 16, feature), half),
            ((3, units, 256, feature), half),
            ((1, units, 256, feature), half),
            ((units, 256, 256), half),
            ((groups, 256, 256), half),
            ((units, feature), full),
            ((1, feature), full),
        ],
        [
            ((n_ctx, feature), full),
            ((n_ctx, 16, feature), half),
            ((1, units, 256, feature), half),
            ((units, 256, 256), half),
        ],
        recv,
        far=(0, 2, 3),
        sems=((3, 8),),
    )
    any_crowded = notes[0, FLAG_LANE]
    back = lax.all_to_all(out_msg, "ctx", 0, 0, tiled=True).reshape(n_ctx * 16, feature)
    scatter = lax.optimization_barrier((row == iota((n_ctx * 16, 1), 0)).astype(half))
    attention = jnp.einsum(
        "rt,rd->td", scatter, back, preferred_element_type=full
    ).reshape(heads, tokens, feature)
    width_all = heads * feature * lax.axis_size("head")
    gain_full = norm_gain[:, None, :]
    scaled_grad = gain_full * upstream.astype(full)
    sums = lax.psum(
        jnp.stack(
            [
                jnp.sum(attention * attention, axis=(0, 2)),
                jnp.sum(scaled_grad * attention, axis=(0, 2)),
                jnp.broadcast_to(any_crowded, (tokens,)),
            ]
        ),
        "head",
    )
    inverse = lax.rsqrt(sums[0] / width_all + 1e-06)[None, :, None]
    dot_total = sums[1][None, :, None]
    grad_attention = (
        inverse * scaled_grad
        - attention * inverse * inverse * inverse * dot_total / width_all
    ).astype(half)
    grad_rows = jnp.einsum(
        "rt,td->rd", scatter, grad_attention.reshape(all_tok, feature),
        preferred_element_type=full,
    ).astype(half)
    grad_recv = lax.all_to_all(
        grad_rows.reshape(n_ctx, 16, feature), "ctx", 0, 0, tiled=True
    )
    (grad_msg,) = call(
        functools.partial(backward_kernel, factor),
        [((n_ctx, 40, feature), half)],
        [((4, units, 256, feature), half)],
        grad_recv, qkv_own, out_own, prob, spread,
    )
    grads_back = lax.all_to_all(grad_msg, "ctx", 0, 0, tiled=True)
    own_sums = own_sums.reshape(heads, per_dev, feature)
    moved = [
        lax.ppermute(
            own_sums[i], "ctx", [(d, (d - HEAD_SHIFT * i) % n_ctx) for d in range(n_ctx)]
        )
        for i in range(1, heads)
    ]
    cluster_sums = jnp.stack([own_sums[0]] + moved, axis=1)
    centroids = cluster_sums * lax.rsqrt(
        jnp.mean(cluster_sums * cluster_sums, axis=2, keepdims=True) + 1e-06
    )
    given = (queries, key_vectors, value_vectors, norm_gain, upstream, cluster_ids, positions)
    shape = (heads, tokens, feature)

    def finish():
        outs = call(
            home_kernel,
            [(shape, half)] * 4,
            [((n_ctx * 16, 3 * feature), half)],
            grads_back, col, attention, inverse.reshape(tokens, 1), norm_gain,
        )
        return (*outs, centroids)

    return lax.cond(sums[2, 0] > 0, lambda: dense(*given), finish)


def solution(mesh):
    tok = P("head", "ctx", None)
    in_specs = (tok, tok, tok, P("head", None), tok, tok, P("ctx"))
    out_specs = (tok, tok, tok, tok, P("ctx", "head", None))
    return jax.shard_map(packed, mesh=mesh, in_specs=in_specs, out_specs=out_specs, check_vma=False)
```

```python
import functools

import jax
import jax.numpy as jnp
from jax import lax
from jax.experimental import pallas as pl
from jax.experimental.pallas import tpu as pltpu
from jax.sharding import PartitionSpec as P

CLUSTERS = 256
SEND_CAP = 2
PACKED = 13
GROUP = 16
HEAD_SHIFT = 32
FLAG_LANE = 48


def rank_within(member):
    tok_count = member.shape[1]
    matches = member[:, :, None] == member[:, None, :]
    earlier = lax.broadcasted_iota(jnp.int32, (tok_count, tok_count), 0) > lax.broadcasted_iota(
        jnp.int32, (tok_count, tok_count), 1
    )
    return jnp.sum(jnp.logical_and(matches, earlier[None]), axis=2, dtype=jnp.int32)


def weights_of(query_block, key_block, slot_pos, factor):
    scores = (
        jnp.einsum("urd,ujd->urj", query_block, key_block, preferred_element_type=jnp.float32)
        * factor
    )
    allowed = jnp.logical_and(
        slot_pos[:, None, :] >= 0, slot_pos[:, None, :] <= slot_pos[:, :, None]
    )
    scores = jnp.where(allowed, scores, -1e30)
    highest = jnp.max(scores, axis=2, keepdims=True)
    exponent = jnp.exp(scores - highest)
    return exponent / jnp.sum(exponent, axis=2, keepdims=True)


def dense(queries, key_vectors, value_vectors, norm_gain, upstream, cluster_ids, positions):
    heads, tokens, feature = queries.shape
    n_ctx = lax.axis_size("ctx")
    per_dev = CLUSTERS // n_ctx
    factor = feature ** (-0.5)
    member = cluster_ids[:, :, 0]
    target = member * SEND_CAP + rank_within(member)
    slots = CLUSTERS * SEND_CAP
    mine = slots // n_ctx
    onehot = (
        target[:, None, :] == lax.broadcasted_iota(jnp.int32, (1, slots, 1), 1)
    )
    place = onehot.astype(jnp.bfloat16)

    def to_owner(source):
        placed = jnp.einsum(
            "hst,htd->hsd", place, source, preferred_element_type=jnp.float32
        ).astype(jnp.bfloat16)
        placed = placed.reshape(heads, n_ctx, mine, source.shape[2])
        placed = placed.transpose(1, 0, 2, 3).reshape(n_ctx, heads * mine, source.shape[2])
        return lax.all_to_all(placed, "ctx", 0, 0, tiled=True)

    def from_owner(block):
        back = lax.all_to_all(block, "ctx", 0, 0, tiled=True)
        back = back.reshape(n_ctx, heads, mine, block.shape[2])
        back = back.transpose(1, 0, 2, 3).reshape(heads, slots, block.shape[2])
        return jnp.einsum(
            "hst,hsd->htd", place, back, preferred_element_type=jnp.float32
        ).astype(jnp.bfloat16)

    def units(recv):
        width = recv.shape[2]
        block = recv.reshape(n_ctx, heads * per_dev, SEND_CAP, width).transpose(1, 0, 2, 3)
        return block.reshape(heads * per_dev, n_ctx * SEND_CAP, width)

    def ununits(block):
        width = block.shape[2]
        recv = block.reshape(heads * per_dev, n_ctx, SEND_CAP, width).transpose(1, 0, 2, 3)
        return recv.reshape(n_ctx, heads * mine, width)

    pos_slots = jnp.sum(
        jnp.where(onehot, positions[None, None, :] + 1, 0), axis=2, dtype=jnp.int32
    ) - 1
    pos_slots = pos_slots.reshape(heads, n_ctx, mine).transpose(1, 0, 2).reshape(n_ctx, heads * mine)
    pos_recv = lax.all_to_all(pos_slots, "ctx", 0, 0, tiled=True)
    slot_pos = units(pos_recv[:, :, None])[:, :, 0]
    recv = to_owner(jnp.concatenate([queries, key_vectors, value_vectors], axis=2))
    block = units(recv)
    query_own, key_own, value_own = (
        block[:, :, :feature], block[:, :, feature : 2 * feature], block[:, :, 2 * feature :]
    )
    weights = weights_of(query_own, key_own, slot_pos, factor)
    rounded = weights.astype(jnp.bfloat16)
    out_own = jnp.einsum(
        "urj,ujd->urd", rounded, value_own, preferred_element_type=jnp.float32
    ).astype(jnp.bfloat16)
    attention = from_owner(ununits(out_own)).astype(jnp.float32)
    width_all = heads * feature * lax.axis_size("head")
    gain_full = norm_gain[:, None, :]
    scaled_grad = gain_full * upstream.astype(jnp.float32)
    sums = lax.psum(
        jnp.stack(
            [
                jnp.sum(attention * attention, axis=(0, 2)),
                jnp.sum(scaled_grad * attention, axis=(0, 2)),
            ]
        ),
        "head",
    )
    inverse = lax.rsqrt(sums[0] / width_all + 1e-06)[None, :, None]
    dot_total = sums[1][None, :, None]
    normed_out = (attention * inverse * gain_full).astype(jnp.bfloat16)
    grad_attention = (
        inverse * scaled_grad
        - attention * inverse * inverse * inverse * dot_total / width_all
    ).astype(jnp.bfloat16)
    grad_block = units(to_owner(grad_attention))
    delta_row = jnp.sum(grad_block.astype(jnp.float32) * out_own.astype(jnp.float32), axis=2)
    grad_value = jnp.einsum(
        "urj,urd->ujd", rounded, grad_block, preferred_element_type=jnp.float32
    ).astype(jnp.bfloat16)
    grad_prob = jnp.einsum(
        "urd,ujd->urj", grad_block, value_own, preferred_element_type=jnp.float32
    )
    grad_score = (factor * weights * (grad_prob - delta_row[:, :, None])).astype(jnp.bfloat16)
    grad_query = jnp.einsum(
        "urj,ujd->urd", grad_score, key_own, preferred_element_type=jnp.float32
    ).astype(jnp.bfloat16)
    grad_key = jnp.einsum(
        "urj,urd->ujd", grad_score, query_own, preferred_element_type=jnp.float32
    ).astype(jnp.bfloat16)
    grads = from_owner(ununits(jnp.concatenate([grad_query, grad_key, grad_value], axis=2)))
    cluster_sums = jnp.sum(key_own.astype(jnp.float32), axis=1)
    cluster_sums = cluster_sums.reshape(heads, per_dev, feature).transpose(1, 0, 2)
    centroids = cluster_sums * lax.rsqrt(
        jnp.mean(cluster_sums * cluster_sums, axis=2, keepdims=True) + 1e-06
    )
    return (
        normed_out,
        grads[:, :, :feature],
        grads[:, :, feature : 2 * feature],
        grads[:, :, 2 * feature :],
        centroids,
    )


def iota(shape, dim):
    return lax.broadcasted_iota(jnp.int32, shape, dim)


def dot(a, b, contract=((1,), (0,))):
    return lax.dot_general(a, b, (contract, ((), ())), preferred_element_type=jnp.float32)


def to_columns(rows):
    width = rows[0].shape[1]
    stacked = jnp.concatenate([r.astype(jnp.float32) for r in rows], axis=0)
    filler = jnp.zeros((128 - len(rows), width), jnp.float32)
    return jnp.transpose(jnp.concatenate([stacked, filler], axis=0))


def to_tiles(rows, note):
    sub = iota((GROUP, 8, 128), 1)
    first, second, third = (r[:, 8:, :] for r in rows)
    third = jnp.where(sub == 5, note, third)
    tile_a = jnp.where(sub < 5, first, pltpu.roll(third, 5, 1))
    tile_b = jnp.where(sub < 5, second, pltpu.roll(third, 2, 1))
    return jnp.concatenate([r[:, :8, :] for r in rows] + [tile_a, tile_b], axis=1)


def from_tiles(message):
    tiles = [message[:, 8 * i : 8 * i + 8, :] for i in range(5)]
    sub = iota((GROUP, 8, 128), 1)
    third = jnp.where(sub < 3, pltpu.roll(tiles[3], 3, 1), pltpu.roll(tiles[4], 6, 1))
    parts = [(tiles[0], tiles[3]), (tiles[1], tiles[4]), (tiles[2], third)]
    rows = [jnp.concatenate(p, axis=1).reshape(GROUP * 16, 128) for p in parts]
    return jnp.concatenate(rows, axis=1).astype(jnp.bfloat16), tiles[4]


def send_kernel(ids_ref, pos_ref, q_ref, k_ref, v_ref, msg_ref, row_ref, col_ref, src_ref):
    heads, _, tokens = ids_ref.shape
    all_tok = heads * tokens
    lane = iota((1, tokens), 1)
    owners, units, orders = [], [], []
    for h in range(heads):
        ids = ids_ref[h]
        owner = ((ids >> 1) + HEAD_SHIFT * h) & 127
        unit = 2 * h + (ids & 1)
        owners.append(owner)
        units.append(unit)
        orders.append((owner * 8 + unit) * tokens + lane)
    order = jnp.concatenate(orders, axis=1)
    owner = jnp.concatenate(owners, axis=1)
    unit = jnp.concatenate(units, axis=1)
    order_col = to_columns([order])[:, 0:1].astype(jnp.int32)
    base = owner * (8 * tokens)
    place = jnp.zeros((1, all_tok), jnp.int32)
    for c in range(all_tok // 128):
        other = order_col[c * 128 : (c + 1) * 128, :]
        hit = jnp.logical_and(other < order, other >= base)
        place = place + jnp.sum(jnp.where(hit, 1, 0), axis=0, keepdims=True)
    ranks = []
    for h in range(heads):
        other = order_col[h * tokens : (h + 1) * tokens, :]
        hit = jnp.logical_and(other < orders[h], other >= orders[h] - lane)
        ranks.append(jnp.sum(jnp.where(hit, 1, 0), axis=0, keepdims=True))
    slot = unit * 2 + jnp.concatenate(ranks, axis=1)
    row = jnp.where(place < PACKED, owner * 16 + place, -1)
    row_ref[...] = row
    crowded = jnp.where(jnp.max(place) >= PACKED, 1.0, 0.0)
    pos = jnp.concatenate([pos_ref[...]] * heads, axis=1)
    cols = to_columns([place, slot + 16, (pos >> 8) + 1, pos & 255, row])
    col_ref[...] = cols[:, 4:5].astype(jnp.int32)
    lanes = iota((all_tok, 128), 1).astype(jnp.float32)
    slot_col = cols[:, 1:2]
    notes = jnp.where(lanes == cols[:, 0:1], slot_col - 15.0, 0.0)
    notes = notes + jnp.where(lanes == slot_col, cols[:, 2:3], 0.0)
    notes = notes + jnp.where(lanes == slot_col + 16.0, cols[:, 3:4], 0.0)
    for i, ref in enumerate((q_ref, k_ref, v_ref)):
        src_ref[:, i * 128 : (i + 1) * 128] = ref[...].reshape(all_tok, 128)
    src_ref[:, 384:512] = notes.astype(jnp.bfloat16)
    flag = jnp.where(iota((1, 1, 128), 2) == FLAG_LANE, crowded, 0.0)

    def step(c):
        at = c * GROUP
        pick = jnp.where(iota((256, all_tok), 0) + at * 16 == row, 1.0, 0.0).astype(jnp.bfloat16)
        got = dot(pick, src_ref[...]).reshape(GROUP, 16, 512)
        rows = [got[:, :, i * 128 : (i + 1) * 128] for i in range(3)]
        note = jnp.sum(got[:, :, 384:512], axis=1, keepdims=True) + flag
        msg_ref[pl.ds(at, GROUP)] = to_tiles(rows, note).astype(jnp.bfloat16)

    for c in range(128 // GROUP):
        step(c)


def put_units(ref, which, at, rows):
    for s in range(16):
        piece = rows[s * GROUP : (s + 1) * GROUP, :]
        ref[which, s // 2, pl.ds((s % 2) * 128 + at, GROUP), :] = piece


def take_units(ref, which, at):
    return jnp.concatenate(
        [ref[which, s // 2, pl.ds((s % 2) * 128 + at, GROUP), :] for s in range(16)], axis=0
    )


def forward_kernel(
    factor, msg_ref, out_msg_ref, qkv_ref, own_ref, prob_ref, spread_ref, sums_ref, flag_ref, note_ref
):
    repeat = (iota((128, 256), 0) == iota((128, 256), 1) % 16).astype(jnp.float32)
    repeat = repeat.astype(jnp.bfloat16)
    r0, r1 = iota((256, 256), 0), iota((256, 256), 1)
    want = (r0 // GROUP + 1).astype(jnp.float32)
    same = r1 // 16 == r0 % GROUP
    sub = iota((GROUP, 8, 128), 1)

    def unpack(g):
        at = g * GROUP
        rows, last = from_tiles(msg_ref[pl.ds(at, GROUP)].astype(jnp.float32))
        note = jnp.sum(jnp.where(sub == 7, last, 0.0), axis=1)
        note_ref[pl.ds(at, GROUP), :] = note
        slot = dot(note.astype(jnp.bfloat16), repeat)
        slot = jnp.concatenate([slot] * 16, axis=0)
        spread = jnp.where(jnp.logical_and(slot == want, same), 1.0, 0.0).astype(jnp.bfloat16)
        spread_ref[g] = spread
        block = dot(spread, rows).astype(jnp.bfloat16)
        for i in range(3):
            put_units(qkv_ref, i, at, block[:, i * 128 : (i + 1) * 128])

    for g in range(128 // GROUP):
        unpack(g)
    note = note_ref[...]
    flag_ref[...] = jnp.max(note, axis=0, keepdims=True)
    pos = jnp.where(note > 0.5, (note - 1.0) * 256.0 + pltpu.roll(note, 112, 1), -1.0)
    pos_t = jnp.transpose(pos)
    for u in range(8):
        a, b = 16 + 2 * u, 17 + 2 * u
        pos_col = jnp.concatenate([pos[:, a : a + 1], pos[:, b : b + 1]], axis=0)
        pos_row = jnp.concatenate([pos_t[a : a + 1, :], pos_t[b : b + 1, :]], axis=1)
        key = qkv_ref[1, u]
        scores = dot(qkv_ref[0, u], key, ((1,), (1,))) * factor
        allowed = jnp.logical_and(pos_row >= 0.0, pos_row <= pos_col)
        scores = jnp.where(allowed, scores, -1e30)
        expo = jnp.exp(scores - jnp.max(scores, axis=1, keepdims=True))
        prob = (expo * (1.0 / jnp.sum(expo, axis=1, keepdims=True))).astype(jnp.bfloat16)
        prob_ref[u] = prob
        own_ref[0, u] = dot(prob, qkv_ref[2, u]).astype(jnp.bfloat16)
        sums_ref[u : u + 1, :] = jnp.sum(key.astype(jnp.float32), axis=0, keepdims=True)

    def pack(g):
        at = g * GROUP
        rows = dot(spread_ref[g], take_units(own_ref, 0, at), ((0,), (0,)))
        out_msg_ref[pl.ds(at, GROUP)] = rows.reshape(GROUP, 16, 128).astype(jnp.bfloat16)

    for g in range(128 // GROUP):
        pack(g)


def backward_kernel(factor, msg_ref, qkv_ref, own_ref, prob_ref, spread_ref, out_msg_ref, grad_ref):
    def unpack(g):
        at = g * GROUP
        rows = msg_ref[pl.ds(at, GROUP)].reshape(GROUP * 16, 128)
        put_units(grad_ref, 0, at, dot(spread_ref[g], rows).astype(jnp.bfloat16))

    for g in range(128 // GROUP):
        unpack(g)
    for u in range(8):
        grad, prob = grad_ref[0, u], prob_ref[u]
        delta = jnp.sum(
            grad.astype(jnp.float32) * own_ref[0, u].astype(jnp.float32), axis=1, keepdims=True
        )
        grad_prob = dot(grad, qkv_ref[2, u], ((1,), (1,)))
        grad_score = (factor * prob.astype(jnp.float32) * (grad_prob - delta)).astype(jnp.bfloat16)
        grad_ref[1, u] = dot(grad_score, qkv_ref[1, u]).astype(jnp.bfloat16)
        grad_ref[2, u] = dot(grad_score, qkv_ref[0, u], ((0,), (0,))).astype(jnp.bfloat16)
        grad_ref[3, u] = dot(prob, grad, ((0,), (0,))).astype(jnp.bfloat16)

    def pack(g):
        at = g * GROUP
        rows = jnp.concatenate([take_units(grad_ref, i, at) for i in (1, 2, 3)], axis=1)
        rows = dot(spread_ref[g], rows, ((0,), (0,))).reshape(GROUP, 16, 384)
        rows = [rows[:, :, i * 128 : (i + 1) * 128] for i in range(3)]
        none = jnp.zeros((GROUP, 1, 128), jnp.float32)
        out_msg_ref[pl.ds(at, GROUP)] = to_tiles(rows, none).astype(jnp.bfloat16)

    for g in range(128 // GROUP):
        pack(g)


def sums_kernel(msg_ref, col_ref, up_ref, gain_ref, note_ref, attn_ref, parts_ref):
    heads, tokens, _ = attn_ref.shape
    rows = msg_ref[...].reshape(2048, 128)
    squares = jnp.zeros((tokens, 128), jnp.float32)
    dots = jnp.zeros((tokens, 128), jnp.float32)
    for h in range(heads):
        col = col_ref[h * tokens : (h + 1) * tokens, :]
        pick = jnp.where(iota((tokens, 2048), 1) == col, 1.0, 0.0).astype(jnp.bfloat16)
        got = dot(pick, rows)
        attn_ref[h] = got.astype(jnp.bfloat16)
        squares = squares + got * got
        dots = dots + gain_ref[h : h + 1, :] * up_ref[h].astype(jnp.float32) * got
    lane = iota((tokens, 128), 1)
    both = jnp.where(lane == 0, jnp.sum(squares, axis=1, keepdims=True), 0.0)
    both = jnp.where(lane == 1, jnp.sum(dots, axis=1, keepdims=True), both)
    flag = jnp.max(jnp.where(iota((1, 128), 1) == FLAG_LANE, note_ref[...], 0.0))
    both = jnp.where(lane == 2, flag, both)
    part = jnp.transpose(both)[:8, :]
    for i in range(parts_ref.shape[0]):
        parts_ref[i] = part


def norm_kernel(
    attn_ref, row_ref, parts_ref, up_ref, gain_ref, msg_ref, inv_ref, flag_ref, src_ref
):
    heads, tokens, _ = attn_ref.shape
    all_tok = heads * tokens
    width_all = 2048.0
    filler = jnp.zeros((120, tokens), jnp.float32)
    sums = jnp.sum(parts_ref[...], axis=0)
    flag_ref[...] = sums[2:3, 0:128]
    cols = jnp.transpose(jnp.concatenate([sums, filler], axis=0))
    inverse = lax.rsqrt(cols[:, 0:1] / width_all + 1e-06)
    inv_ref[...] = inverse
    pull = inverse * inverse * inverse * cols[:, 1:2] / width_all
    for h in range(heads):
        grad = inverse * (gain_ref[h : h + 1, :] * up_ref[h].astype(jnp.float32))
        grad = grad - attn_ref[h].astype(jnp.float32) * pull
        src_ref[h * tokens : (h + 1) * tokens, :] = grad.astype(jnp.bfloat16)
    row = row_ref[...]
    for c in range(128 // GROUP):
        pick = jnp.where(iota((256, all_tok), 0) + c * 256 == row, 1.0, 0.0).astype(jnp.bfloat16)
        got = dot(pick, src_ref[...]).reshape(GROUP, 16, 128)
        msg_ref[c * GROUP : (c + 1) * GROUP] = got.astype(jnp.bfloat16)


def home_kernel(
    msg_ref, col_ref, attn_ref, inv_ref, gain_ref, normed_ref, q_ref, k_ref, v_ref, rows_ref
):
    for g in range(128 // GROUP):
        rows, _ = from_tiles(msg_ref[pl.ds(g * GROUP, GROUP)].astype(jnp.float32))
        rows_ref[g * 256 : (g + 1) * 256, :] = rows
    heads, tokens, _ = q_ref.shape
    for h in range(heads):
        col = col_ref[h * tokens : (h + 1) * tokens, :]
        pick = jnp.where(iota((tokens, 2048), 1) == col, 1.0, 0.0).astype(jnp.bfloat16)
        got = dot(pick, rows_ref[...]).astype(jnp.bfloat16)
        for i, ref in enumerate((q_ref, k_ref, v_ref)):
            ref[h] = got[:, i * 128 : (i + 1) * 128]
        normed = attn_ref[h].astype(jnp.float32) * inv_ref[...] * gain_ref[h : h + 1, :]
        normed_ref[h] = normed.astype(jnp.bfloat16)


def call(kernel, outs, scratch, *args):
    return pl.pallas_call(
        kernel,
        out_shape=[jax.ShapeDtypeStruct(s, t) for s, t in outs],
        scratch_shapes=[pltpu.VMEM(s, t) for s, t in scratch],
        compiler_params=pltpu.CompilerParams(vmem_limit_bytes=28 * 1024 * 1024),
    )(*args)


def packed(queries, key_vectors, value_vectors, norm_gain, upstream, cluster_ids, positions):
    heads, tokens, feature = queries.shape
    n_ctx, n_head = lax.axis_size("ctx"), lax.axis_size("head")
    per_dev = CLUSTERS // n_ctx
    units = heads * per_dev
    groups = n_ctx // GROUP
    factor = feature ** (-0.5)
    all_tok = heads * tokens
    half, full = jnp.bfloat16, jnp.float32
    message, row, col = call(
        send_kernel,
        [
            ((n_ctx, 40, feature), half),
            ((1, all_tok), jnp.int32),
            ((all_tok, 1), jnp.int32),
        ],
        [((all_tok, 4 * feature), half)],
        cluster_ids.reshape(heads, 1, tokens), positions.reshape(1, tokens),
        queries, key_vectors, value_vectors,
    )
    recv = lax.all_to_all(message, "ctx", 0, 0, tiled=True)
    out_msg, qkv_own, out_own, prob, spread, own_sums, notes = call(
        functools.partial(forward_kernel, factor),
        [
            ((n_ctx, 16, feature), half),
            ((3, units, 256, feature), half),
            ((1, units, 256, feature), half),
            ((units, 256, 256), half),
            ((groups, 256, 256), half),
            ((units, feature), full),
            ((1, feature), full),
        ],
        [((n_ctx, feature), full)],
        recv,
    )
    back = lax.all_to_all(out_msg, "ctx", 0, 0, tiled=True)
    shape = (heads, tokens, feature)
    attention, parts = call(
        sums_kernel,
        [(shape, half), ((n_head, 8, tokens), full)],
        [],
        back, col, upstream, norm_gain, notes,
    )
    parts = lax.all_to_all(parts, "head", 0, 0, tiled=True)
    grad_rows, inverse, crowded = call(
        norm_kernel,
        [((n_ctx, 16, feature), half), ((tokens, 1), full), ((1, 128), full)],
        [((all_tok, feature), half)],
        attention, row, parts, upstream, norm_gain,
    )
    grad_recv = lax.all_to_all(
        grad_rows, "ctx", 0, 0, tiled=True
    )
    (grad_msg,) = call(
        functools.partial(backward_kernel, factor),
        [((n_ctx, 40, feature), half)],
        [((4, units, 256, feature), half)],
        grad_recv, qkv_own, out_own, prob, spread,
    )
    grads_back = lax.all_to_all(grad_msg, "ctx", 0, 0, tiled=True)
    own_sums = own_sums.reshape(heads, per_dev, feature)
    moved = [
        lax.ppermute(
            own_sums[i], "ctx", [(d, (d - HEAD_SHIFT * i) % n_ctx) for d in range(n_ctx)]
        )
        for i in range(1, heads)
    ]
    cluster_sums = jnp.stack([own_sums[0]] + moved, axis=1)
    centroids = cluster_sums * lax.rsqrt(
        jnp.mean(cluster_sums * cluster_sums, axis=2, keepdims=True) + 1e-06
    )
    given = (queries, key_vectors, value_vectors, norm_gain, upstream, cluster_ids, positions)
    outs = call(
        home_kernel,
        [(shape, half)] * 4,
        [((n_ctx * 16, 3 * feature), half)],
        grads_back, col, attention, inverse, norm_gain,
    )
    centroids = lax.optimization_barrier(centroids)
    return lax.cond(crowded[0, 0] > 0, lambda: dense(*given), lambda: (*outs, centroids))


def solution(mesh):
    tok = P("head", "ctx", None)
    in_specs = (tok, tok, tok, P("head", None), tok, tok, P("ctx"))
    out_specs = (tok, tok, tok, tok, P("ctx", "head", None))
    return jax.shard_map(packed, mesh=mesh, in_specs=in_specs, out_specs=out_specs, check_vma=False)
```

```python
import functools

import jax
import jax.numpy as jnp
from jax import lax
from jax.experimental import pallas as pl
from jax.experimental.pallas import tpu as pltpu
from jax.sharding import PartitionSpec as P

CLUSTERS = 256
SEND_CAP = 2
PACKED = 13
GROUP = 16
HEAD_SHIFT = 32
FLAG_LANE = 48


def rank_within(member):
    tok_count = member.shape[1]
    matches = member[:, :, None] == member[:, None, :]
    earlier = lax.broadcasted_iota(jnp.int32, (tok_count, tok_count), 0) > lax.broadcasted_iota(
        jnp.int32, (tok_count, tok_count), 1
    )
    return jnp.sum(jnp.logical_and(matches, earlier[None]), axis=2, dtype=jnp.int32)


def weights_of(query_block, key_block, slot_pos, factor):
    scores = (
        jnp.einsum("urd,ujd->urj", query_block, key_block, preferred_element_type=jnp.float32)
        * factor
    )
    allowed = jnp.logical_and(
        slot_pos[:, None, :] >= 0, slot_pos[:, None, :] <= slot_pos[:, :, None]
    )
    scores = jnp.where(allowed, scores, -1e30)
    highest = jnp.max(scores, axis=2, keepdims=True)
    exponent = jnp.exp(scores - highest)
    return exponent / jnp.sum(exponent, axis=2, keepdims=True)


def dense(queries, key_vectors, value_vectors, norm_gain, upstream, cluster_ids, positions):
    heads, tokens, feature = queries.shape
    n_ctx = lax.axis_size("ctx")
    per_dev = CLUSTERS // n_ctx
    factor = feature ** (-0.5)
    member = cluster_ids[:, :, 0]
    target = member * SEND_CAP + rank_within(member)
    slots = CLUSTERS * SEND_CAP
    mine = slots // n_ctx
    onehot = (
        target[:, None, :] == lax.broadcasted_iota(jnp.int32, (1, slots, 1), 1)
    )
    place = onehot.astype(jnp.bfloat16)

    def to_owner(source):
        placed = jnp.einsum(
            "hst,htd->hsd", place, source, preferred_element_type=jnp.float32
        ).astype(jnp.bfloat16)
        placed = placed.reshape(heads, n_ctx, mine, source.shape[2])
        placed = placed.transpose(1, 0, 2, 3).reshape(n_ctx, heads * mine, source.shape[2])
        return lax.all_to_all(placed, "ctx", 0, 0, tiled=True)

    def from_owner(block):
        back = lax.all_to_all(block, "ctx", 0, 0, tiled=True)
        back = back.reshape(n_ctx, heads, mine, block.shape[2])
        back = back.transpose(1, 0, 2, 3).reshape(heads, slots, block.shape[2])
        return jnp.einsum(
            "hst,hsd->htd", place, back, preferred_element_type=jnp.float32
        ).astype(jnp.bfloat16)

    def units(recv):
        width = recv.shape[2]
        block = recv.reshape(n_ctx, heads * per_dev, SEND_CAP, width).transpose(1, 0, 2, 3)
        return block.reshape(heads * per_dev, n_ctx * SEND_CAP, width)

    def ununits(block):
        width = block.shape[2]
        recv = block.reshape(heads * per_dev, n_ctx, SEND_CAP, width).transpose(1, 0, 2, 3)
        return recv.reshape(n_ctx, heads * mine, width)

    pos_slots = jnp.sum(
        jnp.where(onehot, positions[None, None, :] + 1, 0), axis=2, dtype=jnp.int32
    ) - 1
    pos_slots = pos_slots.reshape(heads, n_ctx, mine).transpose(1, 0, 2).reshape(n_ctx, heads * mine)
    pos_recv = lax.all_to_all(pos_slots, "ctx", 0, 0, tiled=True)
    slot_pos = units(pos_recv[:, :, None])[:, :, 0]
    recv = to_owner(jnp.concatenate([queries, key_vectors, value_vectors], axis=2))
    block = units(recv)
    query_own, key_own, value_own = (
        block[:, :, :feature], block[:, :, feature : 2 * feature], block[:, :, 2 * feature :]
    )
    weights = weights_of(query_own, key_own, slot_pos, factor)
    rounded = weights.astype(jnp.bfloat16)
    out_own = jnp.einsum(
        "urj,ujd->urd", rounded, value_own, preferred_element_type=jnp.float32
    ).astype(jnp.bfloat16)
    attention = from_owner(ununits(out_own)).astype(jnp.float32)
    width_all = heads * feature * lax.axis_size("head")
    gain_full = norm_gain[:, None, :]
    scaled_grad = gain_full * upstream.astype(jnp.float32)
    sums = lax.psum(
        jnp.stack(
            [
                jnp.sum(attention * attention, axis=(0, 2)),
                jnp.sum(scaled_grad * attention, axis=(0, 2)),
            ]
        ),
        "head",
    )
    inverse = lax.rsqrt(sums[0] / width_all + 1e-06)[None, :, None]
    dot_total = sums[1][None, :, None]
    normed_out = (attention * inverse * gain_full).astype(jnp.bfloat16)
    grad_attention = (
        inverse * scaled_grad
        - attention * inverse * inverse * inverse * dot_total / width_all
    ).astype(jnp.bfloat16)
    grad_block = units(to_owner(grad_attention))
    delta_row = jnp.sum(grad_block.astype(jnp.float32) * out_own.astype(jnp.float32), axis=2)
    grad_value = jnp.einsum(
        "urj,urd->ujd", rounded, grad_block, preferred_element_type=jnp.float32
    ).astype(jnp.bfloat16)
    grad_prob = jnp.einsum(
        "urd,ujd->urj", grad_block, value_own, preferred_element_type=jnp.float32
    )
    grad_score = (factor * weights * (grad_prob - delta_row[:, :, None])).astype(jnp.bfloat16)
    grad_query = jnp.einsum(
        "urj,ujd->urd", grad_score, key_own, preferred_element_type=jnp.float32
    ).astype(jnp.bfloat16)
    grad_key = jnp.einsum(
        "urj,urd->ujd", grad_score, query_own, preferred_element_type=jnp.float32
    ).astype(jnp.bfloat16)
    grads = from_owner(ununits(jnp.concatenate([grad_query, grad_key, grad_value], axis=2)))
    cluster_sums = jnp.sum(key_own.astype(jnp.float32), axis=1)
    cluster_sums = cluster_sums.reshape(heads, per_dev, feature).transpose(1, 0, 2)
    centroids = cluster_sums * lax.rsqrt(
        jnp.mean(cluster_sums * cluster_sums, axis=2, keepdims=True) + 1e-06
    )
    return (
        normed_out,
        grads[:, :, :feature],
        grads[:, :, feature : 2 * feature],
        grads[:, :, 2 * feature :],
        centroids,
    )


def iota(shape, dim):
    return lax.broadcasted_iota(jnp.int32, shape, dim)


def dot(a, b, contract=((1,), (0,))):
    return lax.dot_general(a, b, (contract, ((), ())), preferred_element_type=jnp.float32)


def to_columns(rows):
    width = rows[0].shape[1]
    stacked = jnp.concatenate([r.astype(jnp.float32) for r in rows], axis=0)
    filler = jnp.zeros((128 - len(rows), width), jnp.float32)
    return jnp.transpose(jnp.concatenate([stacked, filler], axis=0))


def to_tiles(rows, note):
    sub = iota((rows[0].shape[0], 8, 128), 1)
    first, second, third = (r[:, 8:, :] for r in rows)
    third = jnp.where(sub == 5, note, third)
    tile_a = jnp.where(sub < 5, first, pltpu.roll(third, 5, 1))
    tile_b = jnp.where(sub < 5, second, pltpu.roll(third, 2, 1))
    return jnp.concatenate([r[:, :8, :] for r in rows] + [tile_a, tile_b], axis=1)


def from_tiles(message):
    tiles = [message[:, 8 * i : 8 * i + 8, :] for i in range(5)]
    sub = iota((GROUP, 8, 128), 1)
    third = jnp.where(sub < 3, pltpu.roll(tiles[3], 3, 1), pltpu.roll(tiles[4], 6, 1))
    parts = [(tiles[0], tiles[3]), (tiles[1], tiles[4]), (tiles[2], third)]
    rows = [jnp.concatenate(p, axis=1).reshape(GROUP * 16, 128) for p in parts]
    return jnp.concatenate(rows, axis=1).astype(jnp.bfloat16), tiles[4]


def send_kernel(ids_ref, pos_ref, q_ref, k_ref, v_ref, msg_ref, row_ref, col_ref, src_ref):
    heads, _, tokens = ids_ref.shape
    all_tok = heads * tokens
    lane = iota((1, tokens), 1)
    owners, units, orders = [], [], []
    for h in range(heads):
        ids = ids_ref[h]
        owner = ((ids >> 1) + HEAD_SHIFT * h) & 127
        unit = 2 * h + (ids & 1)
        owners.append(owner)
        units.append(unit)
        orders.append((owner * 8 + unit) * tokens + lane)
    order = jnp.concatenate(orders, axis=1)
    owner = jnp.concatenate(owners, axis=1)
    unit = jnp.concatenate(units, axis=1)
    order_col = to_columns([order])[:, 0:1].astype(jnp.int32)
    base = owner * (8 * tokens)
    place = jnp.zeros((1, all_tok), jnp.int32)
    for c in range(all_tok // 128):
        other = order_col[c * 128 : (c + 1) * 128, :]
        hit = jnp.logical_and(other < order, other >= base)
        place = place + jnp.sum(jnp.where(hit, 1, 0), axis=0, keepdims=True)
    ranks = []
    for h in range(heads):
        other = order_col[h * tokens : (h + 1) * tokens, :]
        hit = jnp.logical_and(other < orders[h], other >= orders[h] - lane)
        ranks.append(jnp.sum(jnp.where(hit, 1, 0), axis=0, keepdims=True))
    slot = unit * 2 + jnp.concatenate(ranks, axis=1)
    row = jnp.where(place < PACKED, owner * 16 + place, -1)
    row_ref[...] = row
    crowded = jnp.where(jnp.max(place) >= PACKED, 1.0, 0.0)
    pos = jnp.concatenate([pos_ref[...]] * heads, axis=1)
    cols = to_columns([place, slot + 16, (pos >> 8) + 1, pos & 255, row])
    col_ref[...] = cols[:, 4:5].astype(jnp.int32)
    lanes = iota((all_tok, 128), 1).astype(jnp.float32)
    slot_col = cols[:, 1:2]
    notes = jnp.where(lanes == cols[:, 0:1], slot_col - 15.0, 0.0)
    notes = notes + jnp.where(lanes == slot_col, cols[:, 2:3], 0.0)
    notes = notes + jnp.where(lanes == slot_col + 16.0, cols[:, 3:4], 0.0)
    for i, ref in enumerate((q_ref, k_ref, v_ref)):
        src_ref[:, i * 128 : (i + 1) * 128] = ref[...].reshape(all_tok, 128)
    src_ref[:, 384:512] = notes.astype(jnp.bfloat16)
    flag = jnp.where(iota((1, 1, 128), 2) == FLAG_LANE, crowded, 0.0)

    pick = jnp.where(iota((128 * 16, all_tok), 0) == row, 1.0, 0.0).astype(jnp.bfloat16)
    got = dot(pick, src_ref[...]).reshape(128, 16, 512)
    rows = [got[:, :, i * 128 : (i + 1) * 128] for i in range(3)]
    note = jnp.sum(got[:, :, 384:512], axis=1, keepdims=True) + flag
    msg_ref[...] = to_tiles(rows, note).astype(jnp.bfloat16)


def put_units(ref, which, at, rows):
    for s in range(16):
        piece = rows[s * GROUP : (s + 1) * GROUP, :]
        ref[which, s // 2, pl.ds((s % 2) * 128 + at, GROUP), :] = piece


def take_units(ref, which, at):
    return jnp.concatenate(
        [ref[which, s // 2, pl.ds((s % 2) * 128 + at, GROUP), :] for s in range(16)], axis=0
    )


def forward_kernel(
    factor, msg_ref, out_msg_ref, qkv_ref, own_ref, prob_ref, spread_ref, sums_ref, flag_ref, note_ref
):
    repeat = (iota((128, 256), 0) == iota((128, 256), 1) % 16).astype(jnp.float32)
    repeat = repeat.astype(jnp.bfloat16)
    r0, r1 = iota((256, 256), 0), iota((256, 256), 1)
    want = (r0 // GROUP + 1).astype(jnp.float32)
    same = r1 // 16 == r0 % GROUP
    sub = iota((GROUP, 8, 128), 1)

    def unpack(g):
        at = g * GROUP
        rows, last = from_tiles(msg_ref[pl.ds(at, GROUP)].astype(jnp.float32))
        note = jnp.sum(jnp.where(sub == 7, last, 0.0), axis=1)
        note_ref[pl.ds(at, GROUP), :] = note
        slot = dot(note.astype(jnp.bfloat16), repeat)
        slot = jnp.concatenate([slot] * 16, axis=0)
        spread = jnp.where(jnp.logical_and(slot == want, same), 1.0, 0.0).astype(jnp.bfloat16)
        spread_ref[g] = spread
        block = dot(spread, rows).astype(jnp.bfloat16)
        for i in range(3):
            put_units(qkv_ref, i, at, block[:, i * 128 : (i + 1) * 128])

    for g in range(128 // GROUP):
        unpack(g)
    note = note_ref[...]
    flag_ref[...] = jnp.max(note, axis=0, keepdims=True)
    pos = jnp.where(note > 0.5, (note - 1.0) * 256.0 + pltpu.roll(note, 112, 1), -1.0)
    pos_t = jnp.transpose(pos)
    for u in range(8):
        a, b = 16 + 2 * u, 17 + 2 * u
        pos_col = jnp.concatenate([pos[:, a : a + 1], pos[:, b : b + 1]], axis=0)
        pos_row = jnp.concatenate([pos_t[a : a + 1, :], pos_t[b : b + 1, :]], axis=1)
        key = qkv_ref[1, u]
        scores = dot(qkv_ref[0, u], key, ((1,), (1,))) * factor
        allowed = jnp.logical_and(pos_row >= 0.0, pos_row <= pos_col)
        scores = jnp.where(allowed, scores, -1e30)
        expo = jnp.exp(scores - jnp.max(scores, axis=1, keepdims=True))
        prob = (expo * (1.0 / jnp.sum(expo, axis=1, keepdims=True))).astype(jnp.bfloat16)
        prob_ref[u] = prob
        own_ref[0, u] = dot(prob, qkv_ref[2, u]).astype(jnp.bfloat16)
        sums_ref[u : u + 1, :] = jnp.sum(key.astype(jnp.float32), axis=0, keepdims=True)

    def pack(g):
        at = g * GROUP
        rows = dot(spread_ref[g], take_units(own_ref, 0, at), ((0,), (0,)))
        out_msg_ref[pl.ds(at, GROUP)] = rows.reshape(GROUP, 16, 128).astype(jnp.bfloat16)

    for g in range(128 // GROUP):
        pack(g)


def backward_kernel(factor, msg_ref, qkv_ref, own_ref, prob_ref, spread_ref, out_msg_ref, grad_ref):
    def unpack(g):
        at = g * GROUP
        rows = msg_ref[pl.ds(at, GROUP)].reshape(GROUP * 16, 128)
        put_units(grad_ref, 0, at, dot(spread_ref[g], rows).astype(jnp.bfloat16))

    for g in range(128 // GROUP):
        unpack(g)
    for u in range(8):
        grad, prob = grad_ref[0, u], prob_ref[u]
        delta = jnp.sum(
            grad.astype(jnp.float32) * own_ref[0, u].astype(jnp.float32), axis=1, keepdims=True
        )
        grad_prob = dot(grad, qkv_ref[2, u], ((1,), (1,)))
        grad_score = (factor * prob.astype(jnp.float32) * (grad_prob - delta)).astype(jnp.bfloat16)
        grad_ref[1, u] = dot(grad_score, qkv_ref[1, u]).astype(jnp.bfloat16)
        grad_ref[2, u] = dot(grad_score, qkv_ref[0, u], ((0,), (0,))).astype(jnp.bfloat16)
        grad_ref[3, u] = dot(prob, grad, ((0,), (0,))).astype(jnp.bfloat16)

    def pack(g):
        at = g * GROUP
        rows = jnp.concatenate([take_units(grad_ref, i, at) for i in (1, 2, 3)], axis=1)
        rows = dot(spread_ref[g], rows, ((0,), (0,))).reshape(GROUP, 16, 384)
        rows = [rows[:, :, i * 128 : (i + 1) * 128] for i in range(3)]
        none = jnp.zeros((GROUP, 1, 128), jnp.float32)
        out_msg_ref[pl.ds(at, GROUP)] = to_tiles(rows, none).astype(jnp.bfloat16)

    for g in range(128 // GROUP):
        pack(g)


def sums_kernel(msg_ref, col_ref, up_ref, gain_ref, note_ref, attn_ref, parts_ref):
    heads, tokens, _ = attn_ref.shape
    rows = msg_ref[...].reshape(2048, 128)
    squares = jnp.zeros((tokens, 128), jnp.float32)
    dots = jnp.zeros((tokens, 128), jnp.float32)
    for h in range(heads):
        col = col_ref[h * tokens : (h + 1) * tokens, :]
        pick = jnp.where(iota((tokens, 2048), 1) == col, 1.0, 0.0).astype(jnp.bfloat16)
        got = dot(pick, rows)
        attn_ref[h] = got.astype(jnp.bfloat16)
        squares = squares + got * got
        dots = dots + gain_ref[h : h + 1, :] * up_ref[h].astype(jnp.float32) * got
    lane = iota((tokens, 128), 1)
    both = jnp.where(lane == 0, jnp.sum(squares, axis=1, keepdims=True), 0.0)
    both = jnp.where(lane == 1, jnp.sum(dots, axis=1, keepdims=True), both)
    flag = jnp.max(jnp.where(iota((1, 128), 1) == FLAG_LANE, note_ref[...], 0.0))
    both = jnp.where(lane == 2, flag, both)
    part = jnp.transpose(both)[:8, :]
    for i in range(parts_ref.shape[0]):
        parts_ref[i] = part


def norm_kernel(
    attn_ref, row_ref, parts_ref, up_ref, gain_ref, msg_ref, inv_ref, flag_ref, src_ref
):
    heads, tokens, _ = attn_ref.shape
    all_tok = heads * tokens
    width_all = 2048.0
    filler = jnp.zeros((120, tokens), jnp.float32)
    sums = jnp.sum(parts_ref[...], axis=0)
    flag_ref[...] = sums[2:3, 0:128]
    cols = jnp.transpose(jnp.concatenate([sums, filler], axis=0))
    inverse = lax.rsqrt(cols[:, 0:1] / width_all + 1e-06)
    inv_ref[...] = inverse
    pull = inverse * inverse * inverse * cols[:, 1:2] / width_all
    for h in range(heads):
        grad = inverse * (gain_ref[h : h + 1, :] * up_ref[h].astype(jnp.float32))
        grad = grad - attn_ref[h].astype(jnp.float32) * pull
        src_ref[h * tokens : (h + 1) * tokens, :] = grad.astype(jnp.bfloat16)
    row = row_ref[...]
    for c in range(128 // GROUP):
        pick = jnp.where(iota((256, all_tok), 0) + c * 256 == row, 1.0, 0.0).astype(jnp.bfloat16)
        got = dot(pick, src_ref[...]).reshape(GROUP, 16, 128)
        msg_ref[c * GROUP : (c + 1) * GROUP] = got.astype(jnp.bfloat16)


def home_kernel(
    msg_ref, col_ref, attn_ref, inv_ref, gain_ref, normed_ref, q_ref, k_ref, v_ref, rows_ref
):
    for g in range(128 // GROUP):
        rows, _ = from_tiles(msg_ref[pl.ds(g * GROUP, GROUP)].astype(jnp.float32))
        rows_ref[g * 256 : (g + 1) * 256, :] = rows
    heads, tokens, _ = q_ref.shape
    for h in range(heads):
        col = col_ref[h * tokens : (h + 1) * tokens, :]
        pick = jnp.where(iota((tokens, 2048), 1) == col, 1.0, 0.0).astype(jnp.bfloat16)
        got = dot(pick, rows_ref[...]).astype(jnp.bfloat16)
        for i, ref in enumerate((q_ref, k_ref, v_ref)):
            ref[h] = got[:, i * 128 : (i + 1) * 128]
        normed = attn_ref[h].astype(jnp.float32) * inv_ref[...] * gain_ref[h : h + 1, :]
        normed_ref[h] = normed.astype(jnp.bfloat16)


def call(kernel, outs, scratch, *args):
    return pl.pallas_call(
        kernel,
        out_shape=[jax.ShapeDtypeStruct(s, t) for s, t in outs],
        scratch_shapes=[pltpu.VMEM(s, t) for s, t in scratch],
        compiler_params=pltpu.CompilerParams(vmem_limit_bytes=28 * 1024 * 1024),
    )(*args)


def packed(queries, key_vectors, value_vectors, norm_gain, upstream, cluster_ids, positions):
    heads, tokens, feature = queries.shape
    n_ctx, n_head = lax.axis_size("ctx"), lax.axis_size("head")
    per_dev = CLUSTERS // n_ctx
    units = heads * per_dev
    groups = n_ctx // GROUP
    factor = feature ** (-0.5)
    all_tok = heads * tokens
    half, full = jnp.bfloat16, jnp.float32
    message, row, col = call(
        send_kernel,
        [
            ((n_ctx, 40, feature), half),
            ((1, all_tok), jnp.int32),
            ((all_tok, 1), jnp.int32),
        ],
        [((all_tok, 4 * feature), half)],
        cluster_ids.reshape(heads, 1, tokens), positions.reshape(1, tokens),
        queries, key_vectors, value_vectors,
    )
    recv = lax.all_to_all(message, "ctx", 0, 0, tiled=True)
    out_msg, qkv_own, out_own, prob, spread, own_sums, notes = call(
        functools.partial(forward_kernel, factor),
        [
            ((n_ctx, 16, feature), half),
            ((3, units, 256, feature), half),
            ((1, units, 256, feature), half),
            ((units, 256, 256), half),
            ((groups, 256, 256), half),
            ((units, feature), full),
            ((1, feature), full),
        ],
        [((n_ctx, feature), full)],
        recv,
    )
    back = lax.all_to_all(out_msg, "ctx", 0, 0, tiled=True)
    shape = (heads, tokens, feature)
    attention, parts = call(
        sums_kernel,
        [(shape, half), ((n_head, 8, tokens), full)],
        [],
        back, col, upstream, norm_gain, notes,
    )
    parts = lax.all_to_all(parts, "head", 0, 0, tiled=True)
    grad_rows, inverse, crowded = call(
        norm_kernel,
        [((n_ctx, 16, feature), half), ((tokens, 1), full), ((1, 128), full)],
        [((all_tok, feature), half)],
        attention, row, parts, upstream, norm_gain,
    )
    grad_recv = lax.all_to_all(
        grad_rows, "ctx", 0, 0, tiled=True
    )
    (grad_msg,) = call(
        functools.partial(backward_kernel, factor),
        [((n_ctx, 40, feature), half)],
        [((4, units, 256, feature), half)],
        grad_recv, qkv_own, out_own, prob, spread,
    )
    grads_back = lax.all_to_all(grad_msg, "ctx", 0, 0, tiled=True)
    own_sums = own_sums.reshape(heads, per_dev, feature)
    moved = [
        lax.ppermute(
            own_sums[i], "ctx", [(d, (d - HEAD_SHIFT * i) % n_ctx) for d in range(n_ctx)]
        )
        for i in range(1, heads)
    ]
    cluster_sums = jnp.stack([own_sums[0]] + moved, axis=1)
    centroids = cluster_sums * lax.rsqrt(
        jnp.mean(cluster_sums * cluster_sums, axis=2, keepdims=True) + 1e-06
    )
    given = (queries, key_vectors, value_vectors, norm_gain, upstream, cluster_ids, positions)
    outs = call(
        home_kernel,
        [(shape, half)] * 4,
        [((n_ctx * 16, 3 * feature), half)],
        grads_back, col, attention, inverse, norm_gain,
    )
    centroids = lax.optimization_barrier(centroids)
    return lax.cond(crowded[0, 0] > 0, lambda: dense(*given), lambda: (*outs, centroids))


def solution(mesh):
    tok = P("head", "ctx", None)
    in_specs = (tok, tok, tok, P("head", None), tok, tok, P("ctx"))
    out_specs = (tok, tok, tok, tok, P("ctx", "head", None))
    return jax.shard_map(packed, mesh=mesh, in_specs=in_specs, out_specs=out_specs, check_vma=False)
```

```python
import functools

import jax
import jax.numpy as jnp
from jax import lax
from jax.experimental import pallas as pl
from jax.experimental.pallas import tpu as pltpu
from jax.sharding import PartitionSpec as P

CLUSTERS = 256
SEND_CAP = 2
PACKED = 13
SENT = 14
GROUP = 16
HEAD_SHIFT = 32
FLAG_LANE = 48


def rank_within(member):
    tok_count = member.shape[1]
    matches = member[:, :, None] == member[:, None, :]
    earlier = lax.broadcasted_iota(jnp.int32, (tok_count, tok_count), 0) > lax.broadcasted_iota(
        jnp.int32, (tok_count, tok_count), 1
    )
    return jnp.sum(jnp.logical_and(matches, earlier[None]), axis=2, dtype=jnp.int32)


def weights_of(query_block, key_block, slot_pos, factor):
    scores = (
        jnp.einsum("urd,ujd->urj", query_block, key_block, preferred_element_type=jnp.float32)
        * factor
    )
    allowed = jnp.logical_and(
        slot_pos[:, None, :] >= 0, slot_pos[:, None, :] <= slot_pos[:, :, None]
    )
    scores = jnp.where(allowed, scores, -1e30)
    highest = jnp.max(scores, axis=2, keepdims=True)
    exponent = jnp.exp(scores - highest)
    return exponent / jnp.sum(exponent, axis=2, keepdims=True)


def dense(queries, key_vectors, value_vectors, norm_gain, upstream, cluster_ids, positions):
    heads, tokens, feature = queries.shape
    n_ctx = lax.axis_size("ctx")
    per_dev = CLUSTERS // n_ctx
    factor = feature ** (-0.5)
    member = cluster_ids[:, :, 0]
    target = member * SEND_CAP + rank_within(member)
    slots = CLUSTERS * SEND_CAP
    mine = slots // n_ctx
    onehot = (
        target[:, None, :] == lax.broadcasted_iota(jnp.int32, (1, slots, 1), 1)
    )
    place = onehot.astype(jnp.bfloat16)

    def to_owner(source):
        placed = jnp.einsum(
            "hst,htd->hsd", place, source, preferred_element_type=jnp.float32
        ).astype(jnp.bfloat16)
        placed = placed.reshape(heads, n_ctx, mine, source.shape[2])
        placed = placed.transpose(1, 0, 2, 3).reshape(n_ctx, heads * mine, source.shape[2])
        return lax.all_to_all(placed, "ctx", 0, 0, tiled=True)

    def from_owner(block):
        back = lax.all_to_all(block, "ctx", 0, 0, tiled=True)
        back = back.reshape(n_ctx, heads, mine, block.shape[2])
        back = back.transpose(1, 0, 2, 3).reshape(heads, slots, block.shape[2])
        return jnp.einsum(
            "hst,hsd->htd", place, back, preferred_element_type=jnp.float32
        ).astype(jnp.bfloat16)

    def units(recv):
        width = recv.shape[2]
        block = recv.reshape(n_ctx, heads * per_dev, SEND_CAP, width).transpose(1, 0, 2, 3)
        return block.reshape(heads * per_dev, n_ctx * SEND_CAP, width)

    def ununits(block):
        width = block.shape[2]
        recv = block.reshape(heads * per_dev, n_ctx, SEND_CAP, width).transpose(1, 0, 2, 3)
        return recv.reshape(n_ctx, heads * mine, width)

    pos_slots = jnp.sum(
        jnp.where(onehot, positions[None, None, :] + 1, 0), axis=2, dtype=jnp.int32
    ) - 1
    pos_slots = pos_slots.reshape(heads, n_ctx, mine).transpose(1, 0, 2).reshape(n_ctx, heads * mine)
    pos_recv = lax.all_to_all(pos_slots, "ctx", 0, 0, tiled=True)
    slot_pos = units(pos_recv[:, :, None])[:, :, 0]
    recv = to_owner(jnp.concatenate([queries, key_vectors, value_vectors], axis=2))
    block = units(recv)
    query_own, key_own, value_own = (
        block[:, :, :feature], block[:, :, feature : 2 * feature], block[:, :, 2 * feature :]
    )
    weights = weights_of(query_own, key_own, slot_pos, factor)
    rounded = weights.astype(jnp.bfloat16)
    out_own = jnp.einsum(
        "urj,ujd->urd", rounded, value_own, preferred_element_type=jnp.float32
    ).astype(jnp.bfloat16)
    attention = from_owner(ununits(out_own)).astype(jnp.float32)
    width_all = heads * feature * lax.axis_size("head")
    gain_full = norm_gain[:, None, :]
    scaled_grad = gain_full * upstream.astype(jnp.float32)
    sums = lax.psum(
        jnp.stack(
            [
                jnp.sum(attention * attention, axis=(0, 2)),
                jnp.sum(scaled_grad * attention, axis=(0, 2)),
            ]
        ),
        "head",
    )
    inverse = lax.rsqrt(sums[0] / width_all + 1e-06)[None, :, None]
    dot_total = sums[1][None, :, None]
    normed_out = (attention * inverse * gain_full).astype(jnp.bfloat16)
    grad_attention = (
        inverse * scaled_grad
        - attention * inverse * inverse * inverse * dot_total / width_all
    ).astype(jnp.bfloat16)
    grad_block = units(to_owner(grad_attention))
    delta_row = jnp.sum(grad_block.astype(jnp.float32) * out_own.astype(jnp.float32), axis=2)
    grad_value = jnp.einsum(
        "urj,urd->ujd", rounded, grad_block, preferred_element_type=jnp.float32
    ).astype(jnp.bfloat16)
    grad_prob = jnp.einsum(
        "urd,ujd->urj", grad_block, value_own, preferred_element_type=jnp.float32
    )
    grad_score = (factor * weights * (grad_prob - delta_row[:, :, None])).astype(jnp.bfloat16)
    grad_query = jnp.einsum(
        "urj,ujd->urd", grad_score, key_own, preferred_element_type=jnp.float32
    ).astype(jnp.bfloat16)
    grad_key = jnp.einsum(
        "urj,urd->ujd", grad_score, query_own, preferred_element_type=jnp.float32
    ).astype(jnp.bfloat16)
    grads = from_owner(ununits(jnp.concatenate([grad_query, grad_key, grad_value], axis=2)))
    cluster_sums = jnp.sum(key_own.astype(jnp.float32), axis=1)
    cluster_sums = cluster_sums.reshape(heads, per_dev, feature).transpose(1, 0, 2)
    centroids = cluster_sums * lax.rsqrt(
        jnp.mean(cluster_sums * cluster_sums, axis=2, keepdims=True) + 1e-06
    )
    return (
        normed_out,
        grads[:, :, :feature],
        grads[:, :, feature : 2 * feature],
        grads[:, :, 2 * feature :],
        centroids,
    )


def iota(shape, dim):
    return lax.broadcasted_iota(jnp.int32, shape, dim)


def dot(a, b, contract=((1,), (0,))):
    return lax.dot_general(a, b, (contract, ((), ())), preferred_element_type=jnp.float32)


def to_columns(rows):
    width = rows[0].shape[1]
    stacked = jnp.concatenate([r.astype(jnp.float32) for r in rows], axis=0)
    filler = jnp.zeros((128 - len(rows), width), jnp.float32)
    return jnp.transpose(jnp.concatenate([stacked, filler], axis=0))


def to_tiles(rows, note):
    sub = iota((rows[0].shape[0], 8, 128), 1)
    first, second, third = (r[:, 8:, :] for r in rows)
    third = jnp.where(sub == 5, note, third)
    tile_a = jnp.where(sub < 5, first, pltpu.roll(third, 5, 1))
    tile_b = jnp.where(sub < 5, second, pltpu.roll(third, 2, 1))
    return jnp.concatenate([r[:, :8, :] for r in rows] + [tile_a, tile_b], axis=1)


def from_tiles(message):
    tiles = [message[:, 8 * i : 8 * i + 8, :] for i in range(5)]
    sub = iota((GROUP, 8, 128), 1)
    third = jnp.where(sub < 3, pltpu.roll(tiles[3], 3, 1), pltpu.roll(tiles[4], 6, 1))
    parts = [(tiles[0], tiles[3]), (tiles[1], tiles[4]), (tiles[2], third)]
    rows = [jnp.concatenate(p, axis=1).reshape(GROUP * 16, 128) for p in parts]
    return jnp.concatenate(rows, axis=1).astype(jnp.bfloat16), tiles[4]


def send_kernel(
    ids_ref, pos_ref, q_ref, k_ref, v_ref, msg_ref, row_ref, col_ref, across_ref, src_ref
):
    heads, _, tokens = ids_ref.shape
    all_tok = heads * tokens
    lane = iota((1, tokens), 1)
    owners, units, orders = [], [], []
    for h in range(heads):
        ids = ids_ref[h]
        owner = ((ids >> 1) + HEAD_SHIFT * h) & 127
        unit = 2 * h + (ids & 1)
        owners.append(owner)
        units.append(unit)
        orders.append((owner * 8 + unit) * tokens + lane)
    order = jnp.concatenate(orders, axis=1)
    owner = jnp.concatenate(owners, axis=1)
    unit = jnp.concatenate(units, axis=1)
    order_col = to_columns([order])[:, 0:1].astype(jnp.int32)
    base = owner * (8 * tokens)
    place = jnp.zeros((1, all_tok), jnp.int32)
    for c in range(all_tok // 128):
        other = order_col[c * 128 : (c + 1) * 128, :]
        hit = jnp.logical_and(other < order, other >= base)
        place = place + jnp.sum(jnp.where(hit, 1, 0), axis=0, keepdims=True)
    ranks = []
    for h in range(heads):
        other = order_col[h * tokens : (h + 1) * tokens, :]
        hit = jnp.logical_and(other < orders[h], other >= orders[h] - lane)
        ranks.append(jnp.sum(jnp.where(hit, 1, 0), axis=0, keepdims=True))
    slot = unit * 2 + jnp.concatenate(ranks, axis=1)
    row = jnp.where(place < PACKED, owner * 16 + place, -1)
    across = jnp.where(place < PACKED, place * 128 + owner, -1)
    row_ref[...] = across
    crowded = jnp.where(jnp.max(place) >= PACKED, 1.0, 0.0)
    pos = jnp.concatenate([pos_ref[...]] * heads, axis=1)
    cols = to_columns([place, slot + 16, (pos >> 8) + 1, pos & 255, row, across])
    col_ref[...] = cols[:, 4:5].astype(jnp.int32)
    across_ref[...] = cols[:, 5:6].astype(jnp.int32)
    lanes = iota((all_tok, 128), 1).astype(jnp.float32)
    slot_col = cols[:, 1:2]
    notes = jnp.where(lanes == cols[:, 0:1], slot_col - 15.0, 0.0)
    notes = notes + jnp.where(lanes == slot_col, cols[:, 2:3], 0.0)
    notes = notes + jnp.where(lanes == slot_col + 16.0, cols[:, 3:4], 0.0)
    for i, ref in enumerate((q_ref, k_ref, v_ref)):
        src_ref[:, i * 128 : (i + 1) * 128] = ref[...].reshape(all_tok, 128)
    src_ref[:, 384:512] = notes.astype(jnp.bfloat16)
    flag = jnp.where(iota((1, 1, 128), 2) == FLAG_LANE, crowded, 0.0)

    pick = jnp.where(iota((128 * 16, all_tok), 0) == row, 1.0, 0.0).astype(jnp.bfloat16)
    got = dot(pick, src_ref[...]).reshape(128, 16, 512)
    rows = [got[:, :, i * 128 : (i + 1) * 128] for i in range(3)]
    note = jnp.sum(got[:, :, 384:512], axis=1, keepdims=True) + flag
    msg_ref[...] = to_tiles(rows, note).astype(jnp.bfloat16)


def put_units(ref, which, at, rows):
    for s in range(16):
        piece = rows[s * GROUP : (s + 1) * GROUP, :]
        ref[which, s // 2, pl.ds((s % 2) * 128 + at, GROUP), :] = piece


def take_units(ref, which, at):
    return jnp.concatenate(
        [ref[which, s // 2, pl.ds((s % 2) * 128 + at, GROUP), :] for s in range(16)], axis=0
    )


def forward_kernel(
    factor, msg_ref, out_msg_ref, qkv_ref, own_ref, prob_ref, spread_ref, cross_ref, sums_ref,
    flag_ref, note_ref,
):
    repeat = (iota((128, 256), 0) == iota((128, 256), 1) % 16).astype(jnp.float32)
    repeat = repeat.astype(jnp.bfloat16)
    stretch = (iota((128, 256), 0) == iota((128, 256), 1) // 16).astype(jnp.float32)
    stretch = stretch.astype(jnp.bfloat16)
    same_cross = iota((256, 256), 1) % 16 == iota((256, 256), 0) % GROUP
    r0, r1 = iota((256, 256), 0), iota((256, 256), 1)
    want = (r0 // GROUP + 1).astype(jnp.float32)
    same = r1 // 16 == r0 % GROUP
    sub = iota((GROUP, 8, 128), 1)

    def unpack(g):
        at = g * GROUP
        rows, last = from_tiles(msg_ref[pl.ds(at, GROUP)].astype(jnp.float32))
        note = jnp.sum(jnp.where(sub == 7, last, 0.0), axis=1)
        note_ref[pl.ds(at, GROUP), :] = note
        slot = dot(note.astype(jnp.bfloat16), repeat)
        slot = jnp.concatenate([slot] * 16, axis=0)
        spread = jnp.where(jnp.logical_and(slot == want, same), 1.0, 0.0).astype(jnp.bfloat16)
        spread_ref[g] = spread
        slot = dot(note.astype(jnp.bfloat16), stretch)
        slot = jnp.concatenate([slot] * 16, axis=0)
        cross = jnp.where(jnp.logical_and(slot == want, same_cross), 1.0, 0.0)
        cross_ref[g] = cross.astype(jnp.bfloat16)
        block = dot(spread, rows).astype(jnp.bfloat16)
        for i in range(3):
            put_units(qkv_ref, i, at, block[:, i * 128 : (i + 1) * 128])

    for g in range(128 // GROUP):
        unpack(g)
    note = note_ref[...]
    flag_ref[...] = jnp.max(note, axis=0, keepdims=True)
    pos = jnp.where(note > 0.5, (note - 1.0) * 256.0 + pltpu.roll(note, 112, 1), -1.0)
    pos_t = jnp.transpose(pos)
    for u in range(8):
        a, b = 16 + 2 * u, 17 + 2 * u
        pos_col = jnp.concatenate([pos[:, a : a + 1], pos[:, b : b + 1]], axis=0)
        pos_row = jnp.concatenate([pos_t[a : a + 1, :], pos_t[b : b + 1, :]], axis=1)
        key = qkv_ref[1, u]
        scores = dot(qkv_ref[0, u], key, ((1,), (1,))) * factor
        allowed = jnp.logical_and(pos_row >= 0.0, pos_row <= pos_col)
        scores = jnp.where(allowed, scores, -1e30)
        expo = jnp.exp(scores - jnp.max(scores, axis=1, keepdims=True))
        prob = (expo * (1.0 / jnp.sum(expo, axis=1, keepdims=True))).astype(jnp.bfloat16)
        prob_ref[u] = prob
        own_ref[0, u] = dot(prob, qkv_ref[2, u]).astype(jnp.bfloat16)
        sums_ref[u : u + 1, :] = jnp.sum(key.astype(jnp.float32), axis=0, keepdims=True)

    def pack(g):
        at = g * GROUP
        rows = dot(cross_ref[g], take_units(own_ref, 0, at), ((0,), (0,))).astype(jnp.bfloat16)
        for p in range(SENT):
            out_msg_ref[p, pl.ds(at, GROUP), :] = rows[p * GROUP : (p + 1) * GROUP, :]

    for g in range(128 // GROUP):
        pack(g)


def backward_kernel(
    factor, msg_ref, qkv_ref, own_ref, prob_ref, spread_ref, cross_ref, out_msg_ref, grad_ref
):
    def unpack(g):
        at = g * GROUP
        rows = [msg_ref[p, pl.ds(at, GROUP), :] for p in range(SENT)]
        rows = jnp.concatenate(rows + rows[:2], axis=0)
        put_units(grad_ref, 0, at, dot(cross_ref[g], rows).astype(jnp.bfloat16))

    for g in range(128 // GROUP):
        unpack(g)
    for u in range(8):
        grad, prob = grad_ref[0, u], prob_ref[u]
        delta = jnp.sum(
            grad.astype(jnp.float32) * own_ref[0, u].astype(jnp.float32), axis=1, keepdims=True
        )
        grad_prob = dot(grad, qkv_ref[2, u], ((1,), (1,)))
        grad_score = (factor * prob.astype(jnp.float32) * (grad_prob - delta)).astype(jnp.bfloat16)
        grad_ref[1, u] = dot(grad_score, qkv_ref[1, u]).astype(jnp.bfloat16)
        grad_ref[2, u] = dot(grad_score, qkv_ref[0, u], ((0,), (0,))).astype(jnp.bfloat16)
        grad_ref[3, u] = dot(prob, grad, ((0,), (0,))).astype(jnp.bfloat16)

    def pack(g):
        at = g * GROUP
        rows = jnp.concatenate([take_units(grad_ref, i, at) for i in (1, 2, 3)], axis=1)
        rows = dot(spread_ref[g], rows, ((0,), (0,))).reshape(GROUP, 16, 384)
        rows = [rows[:, :, i * 128 : (i + 1) * 128] for i in range(3)]
        none = jnp.zeros((GROUP, 1, 128), jnp.float32)
        out_msg_ref[pl.ds(at, GROUP)] = to_tiles(rows, none).astype(jnp.bfloat16)

    for g in range(128 // GROUP):
        pack(g)


def sums_kernel(msg_ref, col_ref, up_ref, gain_ref, note_ref, attn_ref, parts_ref):
    heads, tokens, _ = attn_ref.shape
    rows = msg_ref[...].reshape(SENT * 128, 128)
    squares = jnp.zeros((tokens, 128), jnp.float32)
    dots = jnp.zeros((tokens, 128), jnp.float32)
    for h in range(heads):
        col = col_ref[h * tokens : (h + 1) * tokens, :]
        pick = jnp.where(iota((tokens, SENT * 128), 1) == col, 1.0, 0.0).astype(jnp.bfloat16)
        got = dot(pick, rows)
        attn_ref[h] = got.astype(jnp.bfloat16)
        squares = squares + got * got
        dots = dots + gain_ref[h : h + 1, :] * up_ref[h].astype(jnp.float32) * got
    lane = iota((tokens, 128), 1)
    both = jnp.where(lane == 0, jnp.sum(squares, axis=1, keepdims=True), 0.0)
    both = jnp.where(lane == 1, jnp.sum(dots, axis=1, keepdims=True), both)
    flag = jnp.max(jnp.where(iota((1, 128), 1) == FLAG_LANE, note_ref[...], 0.0))
    both = jnp.where(lane == 2, flag, both)
    part = jnp.transpose(both)[:8, :]
    for i in range(parts_ref.shape[0]):
        parts_ref[i] = part


def norm_kernel(
    attn_ref, row_ref, parts_ref, up_ref, gain_ref, msg_ref, inv_ref, flag_ref, src_ref
):
    heads, tokens, _ = attn_ref.shape
    all_tok = heads * tokens
    width_all = 2048.0
    filler = jnp.zeros((120, tokens), jnp.float32)
    sums = jnp.sum(parts_ref[...], axis=0)
    flag_ref[...] = sums[2:3, 0:128]
    cols = jnp.transpose(jnp.concatenate([sums, filler], axis=0))
    inverse = lax.rsqrt(cols[:, 0:1] / width_all + 1e-06)
    inv_ref[...] = inverse
    pull = inverse * inverse * inverse * cols[:, 1:2] / width_all
    for h in range(heads):
        grad = inverse * (gain_ref[h : h + 1, :] * up_ref[h].astype(jnp.float32))
        grad = grad - attn_ref[h].astype(jnp.float32) * pull
        src_ref[h * tokens : (h + 1) * tokens, :] = grad.astype(jnp.bfloat16)
    row = row_ref[...]
    for c in range(SENT // 2):
        pick = jnp.where(iota((256, all_tok), 0) + c * 256 == row, 1.0, 0.0).astype(jnp.bfloat16)
        got = dot(pick, src_ref[...]).reshape(2, 128, 128)
        msg_ref[2 * c : 2 * c + 2] = got.astype(jnp.bfloat16)


def home_kernel(
    msg_ref, col_ref, attn_ref, inv_ref, gain_ref, normed_ref, q_ref, k_ref, v_ref, rows_ref
):
    for g in range(128 // GROUP):
        rows, _ = from_tiles(msg_ref[pl.ds(g * GROUP, GROUP)].astype(jnp.float32))
        rows_ref[g * 256 : (g + 1) * 256, :] = rows
    heads, tokens, _ = q_ref.shape
    for h in range(heads):
        col = col_ref[h * tokens : (h + 1) * tokens, :]
        pick = jnp.where(iota((tokens, 2048), 1) == col, 1.0, 0.0).astype(jnp.bfloat16)
        got = dot(pick, rows_ref[...]).astype(jnp.bfloat16)
        for i, ref in enumerate((q_ref, k_ref, v_ref)):
            ref[h] = got[:, i * 128 : (i + 1) * 128]
        normed = attn_ref[h].astype(jnp.float32) * inv_ref[...] * gain_ref[h : h + 1, :]
        normed_ref[h] = normed.astype(jnp.bfloat16)


def call(kernel, outs, scratch, *args):
    return pl.pallas_call(
        kernel,
        out_shape=[jax.ShapeDtypeStruct(s, t) for s, t in outs],
        scratch_shapes=[pltpu.VMEM(s, t) for s, t in scratch],
        compiler_params=pltpu.CompilerParams(vmem_limit_bytes=28 * 1024 * 1024),
    )(*args)


def packed(queries, key_vectors, value_vectors, norm_gain, upstream, cluster_ids, positions):
    heads, tokens, feature = queries.shape
    n_ctx, n_head = lax.axis_size("ctx"), lax.axis_size("head")
    per_dev = CLUSTERS // n_ctx
    units = heads * per_dev
    groups = n_ctx // GROUP
    factor = feature ** (-0.5)
    all_tok = heads * tokens
    half, full = jnp.bfloat16, jnp.float32
    message, row, col, across = call(
        send_kernel,
        [
            ((n_ctx, 40, feature), half),
            ((1, all_tok), jnp.int32),
            ((all_tok, 1), jnp.int32),
            ((all_tok, 1), jnp.int32),
        ],
        [((all_tok, 4 * feature), half)],
        cluster_ids.reshape(heads, 1, tokens), positions.reshape(1, tokens),
        queries, key_vectors, value_vectors,
    )
    recv = lax.all_to_all(message, "ctx", 0, 0, tiled=True)
    out_msg, qkv_own, out_own, prob, spread, cross, own_sums, notes = call(
        functools.partial(forward_kernel, factor),
        [
            ((SENT, n_ctx, feature), half),
            ((3, units, 256, feature), half),
            ((1, units, 256, feature), half),
            ((units, 256, 256), half),
            ((groups, 256, 256), half),
            ((groups, 256, 256), half),
            ((units, feature), full),
            ((1, feature), full),
        ],
        [((n_ctx, feature), full)],
        recv,
    )
    def exchange(rows):
        pairs = rows.reshape(SENT // 2, 2, n_ctx, feature).transpose(2, 0, 1, 3)
        pairs = lax.all_to_all(pairs, "ctx", 0, 0, tiled=True)
        return pairs.transpose(1, 2, 0, 3).reshape(SENT, n_ctx, feature)

    back = exchange(out_msg)
    shape = (heads, tokens, feature)
    attention, parts = call(
        sums_kernel,
        [(shape, half), ((n_head, 8, tokens), full)],
        [],
        back, across, upstream, norm_gain, notes,
    )
    parts = lax.all_to_all(parts, "head", 0, 0, tiled=True)
    grad_rows, inverse, crowded = call(
        norm_kernel,
        [((SENT, n_ctx, feature), half), ((tokens, 1), full), ((1, 128), full)],
        [((all_tok, feature), half)],
        attention, row, parts, upstream, norm_gain,
    )
    grad_recv = exchange(grad_rows)
    (grad_msg,) = call(
        functools.partial(backward_kernel, factor),
        [((n_ctx, 40, feature), half)],
        [((4, units, 256, feature), half)],
        grad_recv, qkv_own, out_own, prob, spread, cross,
    )
    grads_back = lax.all_to_all(grad_msg, "ctx", 0, 0, tiled=True)
    own_sums = own_sums.reshape(heads, per_dev, feature)
    moved = [
        lax.ppermute(
            own_sums[i], "ctx", [(d, (d - HEAD_SHIFT * i) % n_ctx) for d in range(n_ctx)]
        )
        for i in range(1, heads)
    ]
    cluster_sums = jnp.stack([own_sums[0]] + moved, axis=1)
    centroids = cluster_sums * lax.rsqrt(
        jnp.mean(cluster_sums * cluster_sums, axis=2, keepdims=True) + 1e-06
    )
    given = (queries, key_vectors, value_vectors, norm_gain, upstream, cluster_ids, positions)
    outs = call(
        home_kernel,
        [(shape, half)] * 4,
        [((n_ctx * 16, 3 * feature), half)],
        grads_back, col, attention, inverse, norm_gain,
    )
    centroids = lax.optimization_barrier(centroids)
    return lax.cond(crowded[0, 0] > 0, lambda: dense(*given), lambda: (*outs, centroids))


def solution(mesh):
    tok = P("head", "ctx", None)
    in_specs = (tok, tok, tok, P("head", None), tok, tok, P("ctx"))
    out_specs = (tok, tok, tok, tok, P("ctx", "head", None))
    return jax.shard_map(packed, mesh=mesh, in_specs=in_specs, out_specs=out_specs, check_vma=False)
```

```python
import functools

import jax
import jax.numpy as jnp
from jax import lax
from jax.experimental import pallas as pl
from jax.experimental.pallas import tpu as pltpu
from jax.sharding import PartitionSpec as P

CLUSTERS = 256
SEND_CAP = 2
PACKED = 13
SENT = 14
GROUP = 16
HEAD_SHIFT = 32
FLAG_LANE = 48


def rank_within(member):
    tok_count = member.shape[1]
    matches = member[:, :, None] == member[:, None, :]
    earlier = lax.broadcasted_iota(jnp.int32, (tok_count, tok_count), 0) > lax.broadcasted_iota(
        jnp.int32, (tok_count, tok_count), 1
    )
    return jnp.sum(jnp.logical_and(matches, earlier[None]), axis=2, dtype=jnp.int32)


def weights_of(query_block, key_block, slot_pos, factor):
    scores = (
        jnp.einsum("urd,ujd->urj", query_block, key_block, preferred_element_type=jnp.float32)
        * factor
    )
    allowed = jnp.logical_and(
        slot_pos[:, None, :] >= 0, slot_pos[:, None, :] <= slot_pos[:, :, None]
    )
    scores = jnp.where(allowed, scores, -1e30)
    highest = jnp.max(scores, axis=2, keepdims=True)
    exponent = jnp.exp(scores - highest)
    return exponent / jnp.sum(exponent, axis=2, keepdims=True)


def dense(queries, key_vectors, value_vectors, norm_gain, upstream, cluster_ids, positions):
    heads, tokens, feature = queries.shape
    n_ctx = lax.axis_size("ctx")
    per_dev = CLUSTERS // n_ctx
    factor = feature ** (-0.5)
    member = cluster_ids[:, :, 0]
    target = member * SEND_CAP + rank_within(member)
    slots = CLUSTERS * SEND_CAP
    mine = slots // n_ctx
    onehot = (
        target[:, None, :] == lax.broadcasted_iota(jnp.int32, (1, slots, 1), 1)
    )
    place = onehot.astype(jnp.bfloat16)

    def to_owner(source):
        placed = jnp.einsum(
            "hst,htd->hsd", place, source, preferred_element_type=jnp.float32
        ).astype(jnp.bfloat16)
        placed = placed.reshape(heads, n_ctx, mine, source.shape[2])
        placed = placed.transpose(1, 0, 2, 3).reshape(n_ctx, heads * mine, source.shape[2])
        return lax.all_to_all(placed, "ctx", 0, 0, tiled=True)

    def from_owner(block):
        back = lax.all_to_all(block, "ctx", 0, 0, tiled=True)
        back = back.reshape(n_ctx, heads, mine, block.shape[2])
        back = back.transpose(1, 0, 2, 3).reshape(heads, slots, block.shape[2])
        return jnp.einsum(
            "hst,hsd->htd", place, back, preferred_element_type=jnp.float32
        ).astype(jnp.bfloat16)

    def units(recv):
        width = recv.shape[2]
        block = recv.reshape(n_ctx, heads * per_dev, SEND_CAP, width).transpose(1, 0, 2, 3)
        return block.reshape(heads * per_dev, n_ctx * SEND_CAP, width)

    def ununits(block):
        width = block.shape[2]
        recv = block.reshape(heads * per_dev, n_ctx, SEND_CAP, width).transpose(1, 0, 2, 3)
        return recv.reshape(n_ctx, heads * mine, width)

    pos_slots = jnp.sum(
        jnp.where(onehot, positions[None, None, :] + 1, 0), axis=2, dtype=jnp.int32
    ) - 1
    pos_slots = pos_slots.reshape(heads, n_ctx, mine).transpose(1, 0, 2).reshape(n_ctx, heads * mine)
    pos_recv = lax.all_to_all(pos_slots, "ctx", 0, 0, tiled=True)
    slot_pos = units(pos_recv[:, :, None])[:, :, 0]
    recv = to_owner(jnp.concatenate([queries, key_vectors, value_vectors], axis=2))
    block = units(recv)
    query_own, key_own, value_own = (
        block[:, :, :feature], block[:, :, feature : 2 * feature], block[:, :, 2 * feature :]
    )
    weights = weights_of(query_own, key_own, slot_pos, factor)
    rounded = weights.astype(jnp.bfloat16)
    out_own = jnp.einsum(
        "urj,ujd->urd", rounded, value_own, preferred_element_type=jnp.float32
    ).astype(jnp.bfloat16)
    attention = from_owner(ununits(out_own)).astype(jnp.float32)
    width_all = heads * feature * lax.axis_size("head")
    gain_full = norm_gain[:, None, :]
    scaled_grad = gain_full * upstream.astype(jnp.float32)
    sums = lax.psum(
        jnp.stack(
            [
                jnp.sum(attention * attention, axis=(0, 2)),
                jnp.sum(scaled_grad * attention, axis=(0, 2)),
            ]
        ),
        "head",
    )
    inverse = lax.rsqrt(sums[0] / width_all + 1e-06)[None, :, None]
    dot_total = sums[1][None, :, None]
    normed_out = (attention * inverse * gain_full).astype(jnp.bfloat16)
    grad_attention = (
        inverse * scaled_grad
        - attention * inverse * inverse * inverse * dot_total / width_all
    ).astype(jnp.bfloat16)
    grad_block = units(to_owner(grad_attention))
    delta_row = jnp.sum(grad_block.astype(jnp.float32) * out_own.astype(jnp.float32), axis=2)
    grad_value = jnp.einsum(
        "urj,urd->ujd", rounded, grad_block, preferred_element_type=jnp.float32
    ).astype(jnp.bfloat16)
    grad_prob = jnp.einsum(
        "urd,ujd->urj", grad_block, value_own, preferred_element_type=jnp.float32
    )
    grad_score = (factor * weights * (grad_prob - delta_row[:, :, None])).astype(jnp.bfloat16)
    grad_query = jnp.einsum(
        "urj,ujd->urd", grad_score, key_own, preferred_element_type=jnp.float32
    ).astype(jnp.bfloat16)
    grad_key = jnp.einsum(
        "urj,urd->ujd", grad_score, query_own, preferred_element_type=jnp.float32
    ).astype(jnp.bfloat16)
    grads = from_owner(ununits(jnp.concatenate([grad_query, grad_key, grad_value], axis=2)))
    cluster_sums = jnp.sum(key_own.astype(jnp.float32), axis=1)
    cluster_sums = cluster_sums.reshape(heads, per_dev, feature).transpose(1, 0, 2)
    centroids = cluster_sums * lax.rsqrt(
        jnp.mean(cluster_sums * cluster_sums, axis=2, keepdims=True) + 1e-06
    )
    return (
        normed_out,
        grads[:, :, :feature],
        grads[:, :, feature : 2 * feature],
        grads[:, :, 2 * feature :],
        centroids,
    )


def iota(shape, dim):
    return lax.broadcasted_iota(jnp.int32, shape, dim)


def dot(a, b, contract=((1,), (0,))):
    return lax.dot_general(a, b, (contract, ((), ())), preferred_element_type=jnp.float32)


def to_columns(rows):
    width = rows[0].shape[1]
    stacked = jnp.concatenate([r.astype(jnp.float32) for r in rows], axis=0)
    filler = jnp.zeros((128 - len(rows), width), jnp.float32)
    return jnp.transpose(jnp.concatenate([stacked, filler], axis=0))


def to_tiles(rows, note):
    sub = iota((rows[0].shape[0], 8, 128), 1)
    first, second, third = (r[:, 8:, :] for r in rows)
    third = jnp.where(sub == 5, note, third)
    tile_a = jnp.where(sub < 5, first, pltpu.roll(third, 5, 1))
    tile_b = jnp.where(sub < 5, second, pltpu.roll(third, 2, 1))
    return jnp.concatenate([r[:, :8, :] for r in rows] + [tile_a, tile_b], axis=1)


def from_tiles(message):
    tiles = [message[:, 8 * i : 8 * i + 8, :] for i in range(5)]
    sub = iota((GROUP, 8, 128), 1)
    third = jnp.where(sub < 3, pltpu.roll(tiles[3], 3, 1), pltpu.roll(tiles[4], 6, 1))
    parts = [(tiles[0], tiles[3]), (tiles[1], tiles[4]), (tiles[2], third)]
    rows = [jnp.concatenate(p, axis=1).reshape(GROUP * 16, 128) for p in parts]
    return jnp.concatenate(rows, axis=1).astype(jnp.bfloat16), tiles[4]


def send_kernel(
    ids_ref, pos_ref, q_ref, k_ref, v_ref, msg_ref, row_ref, col_ref, across_ref, src_ref
):
    heads, _, tokens = ids_ref.shape
    all_tok = heads * tokens
    lane = iota((1, tokens), 1)
    owners, units, orders = [], [], []
    for h in range(heads):
        ids = ids_ref[h]
        owner = ((ids >> 1) + HEAD_SHIFT * h) & 127
        unit = 2 * h + (ids & 1)
        owners.append(owner)
        units.append(unit)
        orders.append((owner * 8 + unit) * tokens + lane)
    order = jnp.concatenate(orders, axis=1)
    owner = jnp.concatenate(owners, axis=1)
    unit = jnp.concatenate(units, axis=1)
    order_col = to_columns([order])[:, 0:1].astype(jnp.int32)
    base = owner * (8 * tokens)
    above = (order - base).astype(jnp.uint32)
    place = jnp.zeros((1, all_tok), jnp.int32)
    for c in range(all_tok // 128):
        other = order_col[c * 128 : (c + 1) * 128, :]
        hit = (other - base).astype(jnp.uint32) < above
        place = place + jnp.sum(jnp.where(hit, 1, 0), axis=0, keepdims=True)
    ranks = []
    for h in range(heads):
        other = order_col[h * tokens : (h + 1) * tokens, :]
        hit = jnp.logical_and(other < orders[h], other >= orders[h] - lane)
        ranks.append(jnp.sum(jnp.where(hit, 1, 0), axis=0, keepdims=True))
    slot = unit * 2 + jnp.concatenate(ranks, axis=1)
    row = jnp.where(place < PACKED, owner * 16 + place, -1)
    across = jnp.where(place < PACKED, place * 128 + owner, -1)
    row_ref[...] = across
    crowded = jnp.where(jnp.max(place) >= PACKED, 1.0, 0.0)
    pos = jnp.concatenate([pos_ref[...]] * heads, axis=1)
    cols = to_columns([place, slot + 16, (pos >> 8) + 1, pos & 255, row, across])
    col_ref[...] = cols[:, 4:5].astype(jnp.int32)
    across_ref[...] = cols[:, 5:6].astype(jnp.int32)
    lanes = iota((all_tok, 128), 1).astype(jnp.float32)
    slot_col = cols[:, 1:2]
    notes = jnp.where(lanes == cols[:, 0:1], slot_col - 15.0, 0.0)
    notes = notes + jnp.where(lanes == slot_col, cols[:, 2:3], 0.0)
    notes = notes + jnp.where(lanes == slot_col + 16.0, cols[:, 3:4], 0.0)
    for i, ref in enumerate((q_ref, k_ref, v_ref)):
        src_ref[:, i * 128 : (i + 1) * 128] = ref[...].reshape(all_tok, 128)
    src_ref[:, 384:512] = notes.astype(jnp.bfloat16)
    flag = jnp.where(iota((1, 1, 128), 2) == FLAG_LANE, crowded, 0.0)

    pick = jnp.where(iota((128 * 16, all_tok), 0) == row, 1.0, 0.0).astype(jnp.bfloat16)
    got = dot(pick, src_ref[...]).reshape(128, 16, 512)
    rows = [got[:, :, i * 128 : (i + 1) * 128] for i in range(3)]
    note = jnp.sum(got[:, :, 384:512], axis=1, keepdims=True) + flag
    msg_ref[...] = to_tiles(rows, note).astype(jnp.bfloat16)


def put_units(ref, which, at, rows):
    for s in range(16):
        piece = rows[s * GROUP : (s + 1) * GROUP, :]
        ref[which, s // 2, pl.ds((s % 2) * 128 + at, GROUP), :] = piece


def take_units(ref, which, at):
    return jnp.concatenate(
        [ref[which, s // 2, pl.ds((s % 2) * 128 + at, GROUP), :] for s in range(16)], axis=0
    )


def forward_kernel(
    factor, msg_ref, out_msg_ref, qkv_ref, own_ref, prob_ref, spread_ref, cross_ref, sums_ref,
    flag_ref, note_ref,
):
    repeat = (iota((128, 256), 0) == iota((128, 256), 1) % 16).astype(jnp.float32)
    repeat = repeat.astype(jnp.bfloat16)
    stretch = (iota((128, 256), 0) == iota((128, 256), 1) // 16).astype(jnp.float32)
    stretch = stretch.astype(jnp.bfloat16)
    same_cross = iota((256, 256), 1) % 16 == iota((256, 256), 0) % GROUP
    r0, r1 = iota((256, 256), 0), iota((256, 256), 1)
    want = (r0 // GROUP + 1).astype(jnp.float32)
    same = r1 // 16 == r0 % GROUP
    sub = iota((GROUP, 8, 128), 1)

    def unpack(g):
        at = g * GROUP
        rows, last = from_tiles(msg_ref[pl.ds(at, GROUP)].astype(jnp.float32))
        note = jnp.sum(jnp.where(sub == 7, last, 0.0), axis=1)
        note_ref[pl.ds(at, GROUP), :] = note
        slot = dot(note.astype(jnp.bfloat16), repeat)
        slot = jnp.concatenate([slot] * 16, axis=0)
        spread = jnp.where(jnp.logical_and(slot == want, same), 1.0, 0.0).astype(jnp.bfloat16)
        spread_ref[g] = spread
        slot = dot(note.astype(jnp.bfloat16), stretch)
        slot = jnp.concatenate([slot] * 16, axis=0)
        cross = jnp.where(jnp.logical_and(slot == want, same_cross), 1.0, 0.0)
        cross_ref[g] = cross.astype(jnp.bfloat16)
        block = dot(spread, rows).astype(jnp.bfloat16)
        for i in range(3):
            put_units(qkv_ref, i, at, block[:, i * 128 : (i + 1) * 128])

    for g in range(128 // GROUP):
        unpack(g)
    note = note_ref[...]
    flag_ref[...] = jnp.max(note, axis=0, keepdims=True)
    pos = jnp.where(note > 0.5, (note - 1.0) * 256.0 + pltpu.roll(note, 112, 1), -1.0)
    pos_t = jnp.transpose(pos)
    for u in range(8):
        a, b = 16 + 2 * u, 17 + 2 * u
        pos_col = jnp.concatenate([pos[:, a : a + 1], pos[:, b : b + 1]], axis=0)
        pos_row = jnp.concatenate([pos_t[a : a + 1, :], pos_t[b : b + 1, :]], axis=1)
        key = qkv_ref[1, u]
        scores = dot(qkv_ref[0, u], key, ((1,), (1,))) * factor
        allowed = jnp.logical_and(pos_row >= 0.0, pos_row <= pos_col)
        scores = jnp.where(allowed, scores, -1e30)
        expo = jnp.exp(scores - jnp.max(scores, axis=1, keepdims=True))
        prob = (expo * (1.0 / jnp.sum(expo, axis=1, keepdims=True))).astype(jnp.bfloat16)
        prob_ref[u] = prob
        own_ref[0, u] = dot(prob, qkv_ref[2, u]).astype(jnp.bfloat16)
        sums_ref[u : u + 1, :] = jnp.sum(key.astype(jnp.float32), axis=0, keepdims=True)

    def pack(g):
        at = g * GROUP
        rows = dot(cross_ref[g], take_units(own_ref, 0, at), ((0,), (0,))).astype(jnp.bfloat16)
        for p in range(SENT):
            out_msg_ref[p, pl.ds(at, GROUP), :] = rows[p * GROUP : (p + 1) * GROUP, :]

    for g in range(128 // GROUP):
        pack(g)


def backward_kernel(
    factor, msg_ref, qkv_ref, own_ref, prob_ref, spread_ref, cross_ref, out_msg_ref, grad_ref
):
    def unpack(g):
        at = g * GROUP
        rows = [msg_ref[p, pl.ds(at, GROUP), :] for p in range(SENT)]
        rows = jnp.concatenate(rows + rows[:2], axis=0)
        put_units(grad_ref, 0, at, dot(cross_ref[g], rows).astype(jnp.bfloat16))

    for g in range(128 // GROUP):
        unpack(g)
    for u in range(8):
        grad, prob = grad_ref[0, u], prob_ref[u]
        delta = jnp.sum(
            grad.astype(jnp.float32) * own_ref[0, u].astype(jnp.float32), axis=1, keepdims=True
        )
        grad_prob = dot(grad, qkv_ref[2, u], ((1,), (1,)))
        grad_score = (factor * prob.astype(jnp.float32) * (grad_prob - delta)).astype(jnp.bfloat16)
        grad_ref[1, u] = dot(grad_score, qkv_ref[1, u]).astype(jnp.bfloat16)
        grad_ref[2, u] = dot(grad_score, qkv_ref[0, u], ((0,), (0,))).astype(jnp.bfloat16)
        grad_ref[3, u] = dot(prob, grad, ((0,), (0,))).astype(jnp.bfloat16)

    def pack(g):
        at = g * GROUP
        rows = jnp.concatenate([take_units(grad_ref, i, at) for i in (1, 2, 3)], axis=1)
        rows = dot(spread_ref[g], rows, ((0,), (0,))).reshape(GROUP, 16, 384)
        rows = [rows[:, :, i * 128 : (i + 1) * 128] for i in range(3)]
        none = jnp.zeros((GROUP, 1, 128), jnp.float32)
        out_msg_ref[pl.ds(at, GROUP)] = to_tiles(rows, none).astype(jnp.bfloat16)

    for g in range(128 // GROUP):
        pack(g)


def sums_kernel(msg_ref, col_ref, up_ref, gain_ref, note_ref, attn_ref, parts_ref):
    heads, tokens, _ = attn_ref.shape
    rows = msg_ref[...].reshape(SENT * 128, 128)
    squares = jnp.zeros((tokens, 128), jnp.float32)
    dots = jnp.zeros((tokens, 128), jnp.float32)
    for h in range(heads):
        col = col_ref[h * tokens : (h + 1) * tokens, :]
        pick = jnp.where(iota((tokens, SENT * 128), 1) == col, 1.0, 0.0).astype(jnp.bfloat16)
        got = dot(pick, rows)
        attn_ref[h] = got.astype(jnp.bfloat16)
        squares = squares + got * got
        dots = dots + gain_ref[h : h + 1, :] * up_ref[h].astype(jnp.float32) * got
    lane = iota((tokens, 128), 1)
    both = jnp.where(lane == 0, jnp.sum(squares, axis=1, keepdims=True), 0.0)
    both = jnp.where(lane == 1, jnp.sum(dots, axis=1, keepdims=True), both)
    flag = jnp.max(jnp.where(iota((1, 128), 1) == FLAG_LANE, note_ref[...], 0.0))
    both = jnp.where(lane == 2, flag, both)
    part = jnp.transpose(both)[:8, :]
    for i in range(parts_ref.shape[0]):
        parts_ref[i] = part


def norm_kernel(
    attn_ref, row_ref, parts_ref, up_ref, gain_ref, msg_ref, inv_ref, flag_ref, src_ref
):
    heads, tokens, _ = attn_ref.shape
    all_tok = heads * tokens
    width_all = 2048.0
    filler = jnp.zeros((120, tokens), jnp.float32)
    sums = jnp.sum(parts_ref[...], axis=0)
    flag_ref[...] = sums[2:3, 0:128]
    cols = jnp.transpose(jnp.concatenate([sums, filler], axis=0))
    inverse = lax.rsqrt(cols[:, 0:1] / width_all + 1e-06)
    inv_ref[...] = inverse
    pull = inverse * inverse * inverse * cols[:, 1:2] / width_all
    for h in range(heads):
        grad = inverse * (gain_ref[h : h + 1, :] * up_ref[h].astype(jnp.float32))
        grad = grad - attn_ref[h].astype(jnp.float32) * pull
        src_ref[h * tokens : (h + 1) * tokens, :] = grad.astype(jnp.bfloat16)
    row = row_ref[...]
    for c in range(SENT // 2):
        pick = jnp.where(iota((256, all_tok), 0) + c * 256 == row, 1.0, 0.0).astype(jnp.bfloat16)
        got = dot(pick, src_ref[...]).reshape(2, 128, 128)
        msg_ref[2 * c : 2 * c + 2] = got.astype(jnp.bfloat16)


def home_kernel(
    msg_ref, col_ref, attn_ref, inv_ref, gain_ref, normed_ref, q_ref, k_ref, v_ref, rows_ref
):
    for g in range(128 // GROUP):
        rows, _ = from_tiles(msg_ref[pl.ds(g * GROUP, GROUP)].astype(jnp.float32))
        rows_ref[g * 256 : (g + 1) * 256, :] = rows
    heads, tokens, _ = q_ref.shape
    for h in range(heads):
        col = col_ref[h * tokens : (h + 1) * tokens, :]
        pick = jnp.where(iota((tokens, 2048), 1) == col, 1.0, 0.0).astype(jnp.bfloat16)
        got = dot(pick, rows_ref[...]).astype(jnp.bfloat16)
        for i, ref in enumerate((q_ref, k_ref, v_ref)):
            ref[h] = got[:, i * 128 : (i + 1) * 128]
        normed = attn_ref[h].astype(jnp.float32) * inv_ref[...] * gain_ref[h : h + 1, :]
        normed_ref[h] = normed.astype(jnp.bfloat16)


def call(kernel, outs, scratch, *args):
    return pl.pallas_call(
        kernel,
        out_shape=[jax.ShapeDtypeStruct(s, t) for s, t in outs],
        scratch_shapes=[pltpu.VMEM(s, t) for s, t in scratch],
        compiler_params=pltpu.CompilerParams(vmem_limit_bytes=28 * 1024 * 1024),
    )(*args)


def packed(queries, key_vectors, value_vectors, norm_gain, upstream, cluster_ids, positions):
    heads, tokens, feature = queries.shape
    n_ctx, n_head = lax.axis_size("ctx"), lax.axis_size("head")
    per_dev = CLUSTERS // n_ctx
    units = heads * per_dev
    groups = n_ctx // GROUP
    factor = feature ** (-0.5)
    all_tok = heads * tokens
    half, full = jnp.bfloat16, jnp.float32
    message, row, col, across = call(
        send_kernel,
        [
            ((n_ctx, 40, feature), half),
            ((1, all_tok), jnp.int32),
            ((all_tok, 1), jnp.int32),
            ((all_tok, 1), jnp.int32),
        ],
        [((all_tok, 4 * feature), half)],
        cluster_ids.reshape(heads, 1, tokens), positions.reshape(1, tokens),
        queries, key_vectors, value_vectors,
    )
    recv = lax.all_to_all(message, "ctx", 0, 0, tiled=True)
    out_msg, qkv_own, out_own, prob, spread, cross, own_sums, notes = call(
        functools.partial(forward_kernel, factor),
        [
            ((SENT, n_ctx, feature), half),
            ((3, units, 256, feature), half),
            ((1, units, 256, feature), half),
            ((units, 256, 256), half),
            ((groups, 256, 256), half),
            ((groups, 256, 256), half),
            ((units, feature), full),
            ((1, feature), full),
        ],
        [((n_ctx, feature), full)],
        recv,
    )
    def exchange(rows):
        pairs = rows.reshape(SENT // 2, 2, n_ctx, feature).transpose(2, 0, 1, 3)
        pairs = lax.all_to_all(pairs, "ctx", 0, 0, tiled=True)
        return pairs.transpose(1, 2, 0, 3).reshape(SENT, n_ctx, feature)

    back = exchange(out_msg)
    shape = (heads, tokens, feature)
    attention, parts = call(
        sums_kernel,
        [(shape, half), ((n_head, 8, tokens), full)],
        [],
        back, across, upstream, norm_gain, notes,
    )
    parts = lax.all_to_all(parts, "head", 0, 0, tiled=True)
    grad_rows, inverse, crowded = call(
        norm_kernel,
        [((SENT, n_ctx, feature), half), ((tokens, 1), full), ((1, 128), full)],
        [((all_tok, feature), half)],
        attention, row, parts, upstream, norm_gain,
    )
    grad_recv = exchange(grad_rows)
    (grad_msg,) = call(
        functools.partial(backward_kernel, factor),
        [((n_ctx, 40, feature), half)],
        [((4, units, 256, feature), half)],
        grad_recv, qkv_own, out_own, prob, spread, cross,
    )
    grads_back = lax.all_to_all(grad_msg, "ctx", 0, 0, tiled=True)
    own_sums = own_sums.reshape(heads, per_dev, feature)
    moved = [
        lax.ppermute(
            own_sums[i], "ctx", [(d, (d - HEAD_SHIFT * i) % n_ctx) for d in range(n_ctx)]
        )
        for i in range(1, heads)
    ]
    cluster_sums = jnp.stack([own_sums[0]] + moved, axis=1)
    centroids = cluster_sums * lax.rsqrt(
        jnp.mean(cluster_sums * cluster_sums, axis=2, keepdims=True) + 1e-06
    )
    given = (queries, key_vectors, value_vectors, norm_gain, upstream, cluster_ids, positions)
    outs = call(
        home_kernel,
        [(shape, half)] * 4,
        [((n_ctx * 16, 3 * feature), half)],
        grads_back, col, attention, inverse, norm_gain,
    )
    flat = lax.optimization_barrier(centroids.reshape(units, feature))

    def run_dense():
        *kept, sums = dense(*given)
        return (*kept, sums.reshape(units, feature))

    *kept, flat = lax.cond(crowded[0, 0] > 0, run_dense, lambda: (*outs, flat))
    return (*kept, flat.reshape(per_dev, heads, feature))


def solution(mesh):
    tok = P("head", "ctx", None)
    in_specs = (tok, tok, tok, P("head", None), tok, tok, P("ctx"))
    out_specs = (tok, tok, tok, tok, P("ctx", "head", None))
    return jax.shard_map(packed, mesh=mesh, in_specs=in_specs, out_specs=out_specs, check_vma=False)
```
